32 devices in a mesh: dp: 8 (over y, x, core), expert: 4 (over z).
Axes of the slice: x: 2, y: 2, z: 4, core: 2. Of those that a mesh axis runs over, the one named last changes fastest.
Arguments:
- tokens: bfloat16 [4096, 2560], P(('dp', 'expert')), may hold values from -6 to 6
- cotangent: bfloat16 [4096, 2560], P(('dp', 'expert')), may hold values from -6 to 6
- routes: int32 [4096, 6], P(('dp', 'expert')), may hold values from 0 to 159, all different within a row
- gates: float32 [4096, 6], P(('dp', 'expert')), may hold values from 0.05 to 0.5
- layout: int32 [3, 4], replicated, may hold values from 0 to 3, as said below
- weights: bfloat16 [4, 2560, 768], P('expert', 'dp'), may hold values from -0.125 to 0.125
- first_moment: float32 [4, 2560, 768], P('expert', 'dp'), may hold values from -12 to 12
- second_moment: float32 [4, 2560, 768], P('expert', 'dp'), may hold values from 0.5 to 50
Outputs:
- grad_input: bfloat16 [4096, 2560], P(('dp', 'expert'))
- new_first: float32 [4, 2560, 768], P('expert', 'dp')
- new_second: float32 [4, 2560, 768], P('expert', 'dp')
The draws below stay inside these ranges and needn't reach their ends.
Inputs may be any that keep to these rules, and one draw needn't show every extreme that they name: `routes`: each token names 6 different experts. Row 0 is a permutation of the slots; row 1 is i XOR m for one m of 1 to 3, the same for every i, so that i and layout[1, i] form a pair; row 2 holds 0 or 1, equal for both members of a pair; some pair swaps and, where there are two pairs or more, some pair keeps its slots.
All inputs are finite; a program needn't handle non-finite values.
Results may differ from the reference program's by a relative error of at most 0.015.
Values may be sent and summed in bfloat16 or wider, within the bound.
No kernel may reach another device: no remote copies, remote signals or barrier semaphores. Data moves between devices by JAX's collectives and lax.ppermute only.
A program may use at most 64 MiB of HBM per device.

```python
import math
import jax
import jax.numpy as jnp
from jax import lax

D = 2560
H = 1024
HSPLIT = 4
HD = 256
ROUTED = 160
TOPK = 6
TOK_DEV = 128
CAP = 8
TOKENS = 4096
N_DP = 8
N_EXPERT = 4


def draw_layout(key, part):
    base_key = jax.random.fold_in(key, 7)
    perm_key, mask_key, swap_key, other_key, coin_key = jax.random.split(base_key, 5)
    lane_ids = jnp.arange(N_EXPERT, dtype=jnp.int32)
    placement = jax.random.permutation(perm_key, lane_ids).astype(jnp.int32)
    xor_mask = jax.random.randint(mask_key, (), 1, N_EXPERT, dtype=jnp.int32)
    partner = jnp.bitwise_xor(lane_ids, xor_mask)
    lowest = jnp.minimum(lane_ids, partner)
    coins = jax.random.randint(coin_key, (N_EXPERT,), 0, 2, dtype=jnp.int32)
    swap_lane = jax.random.randint(swap_key, (), 0, N_EXPERT, dtype=jnp.int32)
    other = jax.random.randint(other_key, (), 1, N_EXPERT - 1, dtype=jnp.int32)
    other = other + (other >= xor_mask).astype(jnp.int32)
    keep_lane = jnp.bitwise_xor(swap_lane, other)
    coins = jnp.where(lane_ids == jnp.minimum(swap_lane, jnp.bitwise_xor(swap_lane, xor_mask)), 1, coins)
    coins = jnp.where(lane_ids == jnp.minimum(keep_lane, jnp.bitwise_xor(keep_lane, xor_mask)), 0, coins)
    switch = coins[lowest].astype(jnp.int32)
    return jnp.stack((placement, partner.astype(jnp.int32), switch))


def block_levels(own_key, extent, pieces, low, high):
    factor_of = 1.0
    for dim, blocks in pieces:
        heights = jax.random.uniform(jax.random.fold_in(jax.random.fold_in(own_key, 6), dim), (blocks,), jnp.float32, low / len(pieces), high / len(pieces))
        factor_of = factor_of * jnp.repeat(jnp.exp(heights), extent[dim] // blocks).reshape((-1,) + (1,) * (len(extent) - 1 - dim))
    return factor_of


def picks_of(rng, rows, number_of, top, lift):
    order = jax.random.permutation(jax.random.fold_in(rng, 1), number_of)
    pull = order
    for power in range(3):
        pull = pull * pull // number_of
    pull = pull * lift // number_of
    tickets = jax.random.randint(jax.random.fold_in(rng, 2), (rows, number_of), 0, 4096) + pull
    holders = jax.random.permutation(jax.random.fold_in(rng, 3), rows)[jnp.arange(number_of) % rows]
    tickets = jnp.where(jnp.arange(rows)[:, None] == holders[None, :], 1 << 14, tickets)
    merit = tickets * number_of + jnp.arange(number_of)
    return lax.top_k(merit.astype(jnp.int32), top)[1].astype(jnp.int32)


def noise(stream_key, dims, width, most, cuts=(), kind=jnp.bfloat16):
    drawn = width * jax.random.normal(stream_key, dims, jnp.float32)
    if cuts:
        drawn = drawn * block_levels(stream_key, dims, cuts, -0.22, 0.18)
    return jnp.clip(drawn, -most, most).astype(kind)


def setup_inputs(seed: int = 0) -> dict:
    splits = jax.random.split(jax.random.key(seed), 9)
    return {
        "tokens": noise(splits[0], (TOKENS, D), 1.0, 6.0, ((0, 32),)),
        "cotangent": noise(splits[1], (TOKENS, D), 1.0, 6.0, ((0, 32),)),
        "routes": picks_of(splits[2], TOKENS, ROUTED, TOPK, 307),
        "gates": jnp.clip(jnp.exp(math.log(0.5) - 2.3025851 * jax.random.uniform(splits[3], (TOKENS, TOPK), jnp.float32) ** block_levels(splits[3], (TOKENS, TOPK), ((0, 32),), -0.2, 0.2)), 0.05, 0.5),
        "layout": draw_layout(jax.random.fold_in(splits[8], 71), 0),
        "weights": noise(splits[5], (N_EXPERT, D, 3 * HD), D ** -0.5, 0.125, ((0, 4), (1, 8))),
        "first_moment": noise(splits[6], (N_EXPERT, D, 3 * HD), 2.0, 12.0, ((0, 4), (1, 8)), jnp.float32),
        "second_moment": jnp.clip(jnp.exp(math.log(50.0) - 4.6051702 * jax.random.uniform(splits[7], (N_EXPERT, D, 3 * HD), jnp.float32) ** block_levels(splits[7], (N_EXPERT, D, 3 * HD), ((0, 4), (1, 8)), -0.2, 0.2)), 0.5, 50.0),
    }


first_decay = 0.9
second_decay = 0.999


def rounded(values):
    return lax.optimization_barrier(values.astype(jnp.bfloat16)).astype(jnp.float32)


def take_rows(source, index_rows):
    return source[index_rows]


def add_rows(index_rows, values):
    return jnp.zeros((TOK_DEV + 1, D), jnp.float32).at[index_rows].add(values)


def reference(tokens, cotangent, routes, gates, layout, weights, first_moment, second_moment):
    placement = layout[0]
    xor_mask = layout[1, 0]
    swap_on = layout[2]
    n_block = N_DP * N_EXPERT
    n_window = N_EXPERT // HSPLIT
    width_dev = H // HSPLIT
    per_block = TOK_DEV * TOPK
    route_ids = routes.reshape(n_block, per_block)
    window_ids = jnp.arange(n_window, dtype=jnp.int32)
    hit_table = (route_ids[:, :, None] == window_ids[None, None, :]).astype(jnp.int32)
    earlier = jnp.cumsum(hit_table, axis=1) - hit_table
    position = jnp.sum(earlier * hit_table, axis=2)
    kept = (route_ids < n_window) & (position < CAP)
    slot_key = jnp.where(kept, route_ids * CAP + position, n_window * CAP).astype(jnp.int32)
    token_of = jnp.broadcast_to(jnp.arange(per_block, dtype=jnp.int32) // TOPK, (n_block, per_block))
    block_ids = jnp.broadcast_to(jnp.arange(n_block, dtype=jnp.int32)[:, None], (n_block, per_block))
    token_table = jnp.full((n_block, n_window * CAP + 1), TOK_DEV, dtype=jnp.int32)
    token_table = token_table.at[block_ids, slot_key].set(token_of)[:, :-1]
    gate_table = jnp.zeros((n_block, n_window * CAP + 1), jnp.float32)
    gate_table = gate_table.at[block_ids, slot_key].set(gates.reshape(n_block, per_block).astype(jnp.float32))[:, :-1]
    pad_rows = jnp.zeros((n_block, 1, D), jnp.bfloat16)
    token_blocks = jnp.concatenate((tokens.reshape(n_block, TOK_DEV, D), pad_rows), axis=1)
    cot_blocks = jnp.concatenate((cotangent.reshape(n_block, TOK_DEV, D), pad_rows), axis=1)
    x_buffer = jax.vmap(take_rows)(token_blocks, token_table).reshape(n_block, n_window, CAP, D)
    dy_rows = jax.vmap(take_rows)(cot_blocks, token_table).astype(jnp.float32) * gate_table[:, :, None]
    dy_buffer = dy_rows.astype(jnp.bfloat16).reshape(n_block, n_window, CAP, D)
    lane_ids = jnp.arange(N_EXPERT, dtype=jnp.int32)
    held_slot = jnp.where(swap_on == 1, jnp.bitwise_xor(lane_ids, xor_mask), lane_ids).astype(jnp.int32)
    inverse = jnp.zeros((N_EXPERT,), jnp.int32).at[placement].set(lane_ids)

    def per_slot(dx_total, slot_index):
        expert = (inverse[slot_index] // HSPLIT).astype(jnp.int32)
        w_full = weights[slot_index].astype(jnp.float32)
        rows_in = lax.dynamic_index_in_dim(x_buffer, expert, axis=1, keepdims=False)
        rows_in = rows_in.reshape(N_DP, N_EXPERT * CAP, D).astype(jnp.float32)
        grads_in = lax.dynamic_index_in_dim(dy_buffer, expert, axis=1, keepdims=False)
        grads_in = grads_in.reshape(N_DP, N_EXPERT * CAP, D).astype(jnp.float32)
        pre_act = jnp.einsum('ard,dh->arh', rows_in, w_full[:, :2 * width_dev], precision=lax.Precision.HIGHEST)
        hidden_grad = jnp.einsum('ard,dh->arh', grads_in, w_full[:, 2 * width_dev:], precision=lax.Precision.HIGHEST)
        gate_pre = pre_act[:, :, :width_dev]
        up_pre = pre_act[:, :, width_dev:]
        sigma = jax.nn.sigmoid(gate_pre)
        active_part = gate_pre * sigma
        hidden = rounded(active_part * up_pre)
        gate_grad = rounded(hidden_grad * up_pre * sigma * (1.0 + gate_pre * (1.0 - sigma)))
        up_grad = rounded(hidden_grad * active_part)
        both_grads = jnp.concatenate((gate_grad, up_grad), axis=2)
        part_rows = jnp.einsum('arh,dh->ard', both_grads, w_full[:, :2 * width_dev], precision=lax.Precision.HIGHEST)
        part_rows = rounded(part_rows).reshape(n_block, CAP, D)
        dx_total = dx_total.at[expert].add(part_rows)
        terms = jnp.concatenate((
            jnp.einsum('ard,arh->adh', rows_in, both_grads, precision=lax.Precision.HIGHEST),
            jnp.einsum('ard,arh->adh', grads_in, hidden, precision=lax.Precision.HIGHEST)), axis=2)
        weight_grad = jnp.sum(rounded(terms), axis=0)
        new_first = first_decay * first_moment[slot_index] + (1.0 - first_decay) * weight_grad
        new_second = second_decay * second_moment[slot_index] + (1.0 - second_decay) * weight_grad * weight_grad
        return dx_total, (new_first, new_second)

    start_total = jnp.zeros((n_window, n_block, CAP, D), jnp.float32)
    dx_total, (firsts, seconds) = lax.scan(per_slot, start_total, lane_ids)
    flat_parts = jnp.transpose(dx_total, (1, 0, 2, 3)).reshape(n_block, n_window * CAP, D)
    dx_blocks = jax.vmap(add_rows)(token_table, flat_parts)
    grad_input = dx_blocks[:, :TOK_DEV].reshape(TOKENS, D).astype(jnp.bfloat16)
    return grad_input, firsts[held_slot], seconds[held_slot]
```

```python
import jax
import jax.numpy as jnp
from jax import lax
from jax.sharding import PartitionSpec as P

HSPLIT = 4
CAP = 8


first_decay = 0.9
second_decay = 0.999

BOTH = ("dp", "expert")


def xor_rounds(block, xor_mask):
    count = lax.axis_size("expert")
    for bit_pos in range(count.bit_length() - 1):
        route = [(lane, lane ^ (1 << bit_pos)) for lane in range(count)]
        partner_copy = lax.ppermute(block, "expert", route)
        flip_now = jnp.bitwise_and(jnp.right_shift(xor_mask, bit_pos), 1) == 1
        block = jnp.where(flip_now, partner_copy, block)
    return block


def select_lane(values, lane_ids, index_now):
    return jnp.sum(jnp.where(lane_ids == index_now, values, 0))


def exchange(block, axes):
    return lax.all_to_all(block, axes, split_axis=0, concat_axis=0, tiled=True)


def body(move, active, tokens, cotangent, routes, gates, expert_at, weights, first_moment, second_moment):
    n_expert = lax.axis_size("expert")
    n_dp = lax.axis_size("dp")
    n_window = n_expert // HSPLIT
    tok_dev, top_count = routes.shape
    width = tokens.shape[1]
    depth = weights.shape[1]
    width_dev = weights.shape[2] // 3
    bf16 = jnp.bfloat16

    held_weights = jnp.where(active, move(weights[0]), weights[0])

    flat_ids = routes.reshape(-1)
    window_ids = jnp.arange(n_window, dtype=jnp.int32)
    hit_table = (flat_ids[:, None] == window_ids[None, :]).astype(jnp.int32)
    earlier = jnp.cumsum(hit_table, axis=0) - hit_table
    position = jnp.sum(earlier * hit_table, axis=1)
    kept = (flat_ids < n_window) & (position < CAP)
    slot_key = jnp.where(kept, flat_ids * CAP + position, -1)
    slot_pick = (jnp.arange(n_window * CAP, dtype=jnp.int32)[:, None] == slot_key[None, :]).astype(
        jnp.float32
    )
    assign_pick = slot_pick.reshape(n_window * CAP, tok_dev, top_count)
    slot_token = jnp.sum(assign_pick, axis=2)
    slot_gate = jnp.sum(assign_pick * gates[None], axis=(1, 2))[:, None]
    rows = jnp.dot(slot_token.astype(bf16), tokens, preferred_element_type=jnp.float32).astype(bf16)
    grads = jnp.dot(slot_token.astype(bf16), cotangent, preferred_element_type=jnp.float32)
    grads = (grads * slot_gate).astype(bf16)
    sends = jnp.stack((rows, grads)).reshape(2, n_window, CAP, n_dp, depth).transpose(3, 1, 0, 2, 4)
    if n_window == 1:
        sends = jnp.broadcast_to(sends, (n_dp, n_expert, 2, CAP, depth))
        dest_token = jnp.broadcast_to(slot_token[None], (n_expert, CAP, tok_dev))
    else:
        sends = jnp.take(sends, expert_at, axis=1)
        dest_token = jnp.take(slot_token.reshape(n_window, CAP, tok_dev), expert_at, axis=0)
    dest_token = dest_token.reshape(n_expert * CAP, tok_dev).astype(bf16)
    got = exchange(sends.reshape(n_dp * n_expert, 2, CAP, depth), BOTH)
    rows_in = got[:, 0].reshape(-1, depth)
    grads_in = got[:, 1].reshape(-1, depth)

    pre_part = jnp.dot(rows_in, held_weights[:, : 2 * width_dev], preferred_element_type=jnp.float32)
    grad_part = jnp.dot(grads_in, held_weights[:, 2 * width_dev :], preferred_element_type=jnp.float32)
    parts = jnp.concatenate((pre_part, grad_part), axis=1).astype(bf16)
    sums = exchange(parts.reshape(n_dp, n_expert * CAP, 3 * width_dev), "dp")
    sums = jnp.sum(sums.astype(jnp.float32), axis=0)
    gate_pre = sums[:, :width_dev]
    up_pre = sums[:, width_dev : 2 * width_dev]
    hidden_grad = sums[:, 2 * width_dev :]
    sigma = jax.nn.sigmoid(gate_pre)
    active_part = gate_pre * sigma
    hidden = active_part * up_pre
    gate_grad = hidden_grad * up_pre * sigma * (1.0 + gate_pre * (1.0 - sigma))
    up_grad = hidden_grad * active_part
    acts = jnp.concatenate((gate_grad, up_grad, hidden), axis=1).astype(bf16)
    acts = lax.all_gather(acts, "dp", axis=0, tiled=True)
    both_grads = acts[:, : 2 * width_dev]
    part_rows = lax.dot_general(
        both_grads,
        held_weights[:, : 2 * width_dev],
        (((1,), (1,)), ((), ())),
        preferred_element_type=jnp.float32,
    ).astype(bf16)
    returned = exchange(part_rows.reshape(n_dp * n_expert, CAP, depth), BOTH)
    returned = returned.reshape(n_dp, n_expert * CAP, depth).transpose(1, 0, 2).reshape(-1, width)
    grad_input = lax.dot_general(
        dest_token, returned, (((0,), (0,)), ((), ())), preferred_element_type=jnp.float32
    ).astype(bf16)

    proj_grad = lax.dot_general(
        rows_in, both_grads, (((0,), (0,)), ((), ())), preferred_element_type=jnp.float32
    )
    down_grad = lax.dot_general(
        grads_in, acts[:, 2 * width_dev :], (((0,), (0,)), ((), ())), preferred_element_type=jnp.float32
    )
    weight_grad = jnp.concatenate((proj_grad, down_grad), axis=1)
    moments = jnp.stack((first_moment[0], second_moment[0]))
    moved = move(moments.astype(bf16)).astype(jnp.float32)
    moments = jnp.where(active, moved, moments)
    new_first = first_decay * moments[0] + (1.0 - first_decay) * weight_grad
    new_second = second_decay * moments[1] + (1.0 - second_decay) * weight_grad * weight_grad
    return grad_input, new_first[None], new_second[None]


def local(tokens, cotangent, routes, gates, layout, weights, first_moment, second_moment):
    n_expert = lax.axis_size("expert")
    own_index = lax.axis_index("expert")
    lane_ids = jnp.arange(n_expert, dtype=jnp.int32)
    placement = layout[0]
    xor_mask = layout[1, 0]
    swap_on = layout[2]
    held_slot = jnp.where(swap_on == 1, jnp.bitwise_xor(lane_ids, xor_mask), lane_ids)
    inverse = jnp.sum(
        jnp.where(placement[None, :] == lane_ids[:, None], lane_ids[None, :], 0), axis=1
    )
    slot_owner = inverse // HSPLIT
    expert_at = jnp.sum(
        jnp.where(held_slot[:, None] == lane_ids[None, :], slot_owner[None, :], 0), axis=1
    )
    args = (tokens, cotangent, routes, gates, expert_at, weights, first_moment, second_moment)
    if n_expert != 4:
        active = select_lane(swap_on, lane_ids, own_index) == 1
        return body(lambda block: xor_rounds(block, xor_mask), active, *args)
    pairs = [(low, high) for low in range(4) for high in range(low + 1, 4)]

    def branch(pair):
        low, high = pair

        def run(*operands):
            active = (own_index == low) | (own_index == high)
            move = lambda block: lax.ppermute(block, "expert", [(low, high), (high, low)])
            return body(move, active, *operands)

        return run

    case = jnp.int32(0)
    for number, (low, high) in enumerate(pairs):
        case = case + number * ((swap_on[low] == 1) & (xor_mask == low ^ high)).astype(jnp.int32)
    return lax.switch(case, [branch(pair) for pair in pairs], *args)


def solution(mesh):
    in_specs = (
        P(BOTH, None),
        P(BOTH, None),
        P(BOTH, None),
        P(BOTH, None),
        P(),
        P("expert", "dp", None),
        P("expert", "dp", None),
        P("expert", "dp", None),
    )
    out_specs = (P(BOTH, None), P("expert", "dp", None), P("expert", "dp", None))
    return jax.shard_map(local, mesh=mesh, in_specs=in_specs, out_specs=out_specs, check_vma=False)
```

```python
import jax
import jax.numpy as jnp
from jax import lax
from jax.sharding import Mesh, PartitionSpec as P

HSPLIT = 4
CAP = 8


first_decay = 0.9
second_decay = 0.999

DP = ("outer", "inner", "core")
CHIPS = ("outer", "inner")
ROWS = DP + ("expert",)


def xor_rounds(block, xor_mask):
    count = lax.axis_size("expert")
    for bit_pos in range(count.bit_length() - 1):
        route = [(lane, lane ^ (1 << bit_pos)) for lane in range(count)]
        partner_copy = lax.ppermute(block, "expert", route)
        flip_now = jnp.bitwise_and(jnp.right_shift(xor_mask, bit_pos), 1) == 1
        block = jnp.where(flip_now, partner_copy, block)
    return block


def select_lane(values, lane_ids, index_now):
    return jnp.sum(jnp.where(lane_ids == index_now, values, 0))


def exchange(block, axes):
    return lax.all_to_all(block, axes, split_axis=0, concat_axis=0, tiled=True)


def body(move, active, tokens, cotangent, routes, gates, expert_at, weights, first_moment, second_moment):
    n_expert = lax.axis_size("expert")
    n_chip = lax.axis_size(CHIPS)
    n_window = n_expert // HSPLIT
    tok_dev, top_count = routes.shape
    width = tokens.shape[1]
    own_depth = weights.shape[1]
    depth = 2 * own_depth
    width_dev = weights.shape[2] // 3
    bf16 = jnp.bfloat16
    core = lax.axis_index("core")

    block = weights[0]
    if n_window > 1:
        block = jnp.where(active, move(block), block)
    chip_weights = lax.all_gather(block, "core", axis=0, tiled=True)

    flat_ids = routes.reshape(-1)
    window_ids = jnp.arange(n_window, dtype=jnp.int32)
    hit_table = (flat_ids[:, None] == window_ids[None, :]).astype(jnp.int32)
    earlier = jnp.cumsum(hit_table, axis=0) - hit_table
    position = jnp.sum(earlier * hit_table, axis=1)
    kept = (flat_ids < n_window) & (position < CAP)
    slot_key = jnp.where(kept, flat_ids * CAP + position, -1)
    slot_pick = (jnp.arange(n_window * CAP, dtype=jnp.int32)[:, None] == slot_key[None, :]).astype(
        jnp.float32
    )
    assign_pick = slot_pick.reshape(n_window * CAP, tok_dev, top_count)
    slot_token = jnp.sum(assign_pick, axis=2)
    slot_gate = jnp.sum(assign_pick * gates[None], axis=(1, 2))[:, None]
    rows = jnp.dot(slot_token.astype(bf16), tokens, preferred_element_type=jnp.float32).astype(bf16)
    grads = jnp.dot(slot_token.astype(bf16), cotangent, preferred_element_type=jnp.float32)
    grads = (grads * slot_gate).astype(bf16)
    sends = jnp.stack((rows, grads)).reshape(2, n_window, CAP, n_chip, depth).transpose(3, 1, 0, 2, 4)
    if n_window == 1:
        sends = jnp.broadcast_to(sends, (n_chip, n_expert, 2, CAP, depth))
        dest_token = jnp.broadcast_to(slot_token[None], (n_expert, CAP, tok_dev))
    else:
        sends = jnp.take(sends, expert_at, axis=1)
        dest_token = jnp.take(slot_token.reshape(n_window, CAP, tok_dev), expert_at, axis=0)
    dest_token = dest_token.reshape(n_expert * CAP, tok_dev).astype(bf16)
    got = exchange(sends.reshape(n_chip * n_expert, 2, CAP, depth), CHIPS + ("expert",))
    rows_in = got[:, 0].reshape(-1, depth)
    grads_in = got[:, 1].reshape(-1, depth)

    pre_part = jnp.dot(rows_in, chip_weights[:, : 2 * width_dev], preferred_element_type=jnp.float32)
    grad_part = jnp.dot(grads_in, chip_weights[:, 2 * width_dev :], preferred_element_type=jnp.float32)
    parts = jnp.concatenate((pre_part, grad_part), axis=1).astype(bf16)
    if n_chip > 4:
        sums = exchange(parts.reshape(n_chip, -1, parts.shape[1]), CHIPS)
        sums = jnp.sum(sums.astype(jnp.float32), axis=0).astype(bf16)
        sums = lax.all_gather(sums, CHIPS, axis=0, tiled=True).astype(jnp.float32)
    else:
        sums = jnp.sum(lax.all_gather(parts, CHIPS, axis=0).astype(jnp.float32), axis=0)
    gate_pre = sums[:, :width_dev]
    up_pre = sums[:, width_dev : 2 * width_dev]
    hidden_grad = sums[:, 2 * width_dev :]
    sigma = jax.nn.sigmoid(gate_pre)
    active_part = gate_pre * sigma
    hidden = active_part * up_pre
    gate_grad = hidden_grad * up_pre * sigma * (1.0 + gate_pre * (1.0 - sigma))
    up_grad = hidden_grad * active_part
    acts = jnp.concatenate((gate_grad, up_grad, hidden), axis=1).astype(bf16)
    part_rows = lax.dot_general(
        acts[:, : 2 * width_dev],
        chip_weights[:, : 2 * width_dev],
        (((1,), (1,)), ((), ())),
        preferred_element_type=jnp.float32,
    ).astype(bf16)
    returned = exchange(part_rows.reshape(n_chip * n_expert, CAP, depth), CHIPS + ("expert",))
    returned = returned.reshape(n_chip, n_expert * CAP, depth).transpose(1, 0, 2).reshape(-1, width)
    grad_input = lax.dot_general(
        dest_token, returned, (((0,), (0,)), ((), ())), preferred_element_type=jnp.float32
    ).astype(bf16)

    if n_window == 1:
        acts = jnp.where(active, move(acts), acts)
    proj_grad = lax.dot_general(
        rows_in, acts[:, : 2 * width_dev], (((0,), (0,)), ((), ())), preferred_element_type=jnp.float32
    )
    down_grad = lax.dot_general(
        grads_in, acts[:, 2 * width_dev :], (((0,), (0,)), ((), ())), preferred_element_type=jnp.float32
    )
    weight_grad = jnp.concatenate((proj_grad, down_grad), axis=1)
    low, high = weight_grad[:own_depth], weight_grad[own_depth:]
    other = lax.ppermute(jnp.where(core == 0, high, low).astype(bf16), "core", [(0, 1), (1, 0)])
    weight_grad = jnp.where(core == 0, low, high) + other.astype(jnp.float32)
    moments = jnp.stack((first_moment[0], second_moment[0]))
    moved = move(moments.astype(bf16)).astype(jnp.float32)
    moments = jnp.where(active, moved, moments)
    new_first = first_decay * moments[0] + (1.0 - first_decay) * weight_grad
    new_second = second_decay * moments[1] + (1.0 - second_decay) * weight_grad * weight_grad
    return grad_input, new_first[None], new_second[None]


def local(tokens, cotangent, routes, gates, layout, weights, first_moment, second_moment):
    n_expert = lax.axis_size("expert")
    own_index = lax.axis_index("expert")
    args = (tokens, cotangent, routes, gates)
    rest = (weights, first_moment, second_moment)
    swap_on = layout[2]
    if n_expert != 4:
        lane_ids = jnp.arange(n_expert, dtype=jnp.int32)
        placement = layout[0]
        xor_mask = layout[1, 0]
        held_slot = jnp.where(swap_on == 1, jnp.bitwise_xor(lane_ids, xor_mask), lane_ids)
        inverse = jnp.sum(
            jnp.where(placement[None, :] == lane_ids[:, None], lane_ids[None, :], 0), axis=1
        )
        slot_owner = inverse // HSPLIT
        expert_at = jnp.sum(
            jnp.where(held_slot[:, None] == lane_ids[None, :], slot_owner[None, :], 0), axis=1
        )
        active = select_lane(swap_on, lane_ids, own_index) == 1
        return body(lambda block: xor_rounds(block, xor_mask), active, *args, expert_at, *rest)
    pairs = [(low, high) for low in range(4) for high in range(low + 1, 4)]

    def branch(pair):
        low, high = pair

        def run(*operands):
            active = (own_index == low) | (own_index == high)
            move = lambda block: lax.ppermute(block, "expert", [(low, high), (high, low)])
            return body(move, active, *operands[:4], None, *operands[4:])

        return run

    case = jnp.sum(swap_on * jnp.array([-1, 1, 2, 3], dtype=jnp.int32))
    return lax.switch(case, [branch(pair) for pair in pairs], *args, *rest)


def solution(mesh):
    n_dp, n_expert = mesh.devices.shape
    split = Mesh(mesh.devices.reshape(n_dp // 4, 2, 2, n_expert), ROWS)
    in_specs = (
        P(ROWS, None),
        P(ROWS, None),
        P(ROWS, None),
        P(ROWS, None),
        P(),
        P("expert", DP, None),
        P("expert", DP, None),
        P("expert", DP, None),
    )
    out_specs = (P(ROWS, None), P("expert", DP, None), P("expert", DP, None))
    return jax.shard_map(local, mesh=split, in_specs=in_specs, out_specs=out_specs, check_vma=False)
```

```python
import functools

import jax
import jax.numpy as jnp
from jax import lax
from jax.experimental import pallas as pl
from jax.experimental.pallas import tpu as pltpu
from jax.sharding import Mesh, PartitionSpec as P

HSPLIT = 4
CAP = 8


first_decay = 0.9
second_decay = 0.999

DP = ("outer", "inner", "core")
CHIPS = ("outer", "inner")
ROWS = DP + ("expert",)
ACROSS = CHIPS + ("expert",)
PAIRS = [(low, high) for low in range(4) for high in range(low + 1, 4)]
CUTS = (20, 30)


def xor_rounds(block, xor_mask):
    count = lax.axis_size("expert")
    for bit_pos in range(count.bit_length() - 1):
        route = [(lane, lane ^ (1 << bit_pos)) for lane in range(count)]
        partner_copy = lax.ppermute(block, "expert", route)
        flip_now = jnp.bitwise_and(jnp.right_shift(xor_mask, bit_pos), 1) == 1
        block = jnp.where(flip_now, partner_copy, block)
    return block


def select_lane(values, lane_ids, index_now):
    return jnp.sum(jnp.where(lane_ids == index_now, values, 0))


def exchange(block, axes):
    return lax.all_to_all(block, axes, split_axis=0, concat_axis=0, tiled=True)


def pick_kernel(layout_ref, routes_ref, gates_ref, tokens_ref, cot_ref, case_ref, sends_ref, pick_ref):
    n_chip, n_expert, _, depth = sends_ref.shape
    tok_dev = tokens_ref.shape[0]
    case_ref[0, 0] = layout_ref[2, 1] - layout_ref[2, 0] + 2 * layout_ref[2, 2] + 3 * layout_ref[2, 3]
    hit = jnp.where(routes_ref[...] == 0, 1.0, 0.0)
    gate = jnp.sum(hit * gates_ref[...], axis=0, keepdims=True)
    hit = jnp.broadcast_to(jnp.sum(hit, axis=0, keepdims=True), (CAP, tok_dev))
    row_ids = lax.broadcasted_iota(jnp.int32, (tok_dev, tok_dev), 0)
    col_ids = lax.broadcasted_iota(jnp.int32, (tok_dev, tok_dev), 1)
    before = jnp.where(row_ids < col_ids, 1.0, 0.0).astype(jnp.bfloat16)
    position = jnp.dot(hit.astype(jnp.bfloat16), before, preferred_element_type=jnp.float32)
    slots = lax.broadcasted_iota(jnp.int32, (CAP, tok_dev), 0).astype(jnp.float32)
    pick = jnp.where(position == slots, hit, 0.0)
    slot_gate = jnp.sum(pick * gate, axis=1, keepdims=True)
    pick = pick.astype(jnp.bfloat16)
    pick_ref[...] = pick
    for chip in range(n_chip):
        span = slice(chip * depth, (chip + 1) * depth)
        rows = jnp.dot(pick, tokens_ref[:, span], preferred_element_type=jnp.float32)
        grads = jnp.dot(pick, cot_ref[:, span], preferred_element_type=jnp.float32) * slot_gate
        both = jnp.concatenate((rows, grads), axis=0).astype(jnp.bfloat16)
        for expert in range(n_expert):
            sends_ref[chip, expert] = both


def pick_rows(layout, routes, gates, tokens, cotangent):
    tok_dev, width = tokens.shape
    n_chip, n_expert = lax.axis_size(CHIPS), lax.axis_size("expert")
    vmem = pl.BlockSpec(memory_space=pltpu.VMEM)
    smem = pl.BlockSpec(memory_space=pltpu.SMEM)
    return pl.pallas_call(
        pick_kernel,
        out_shape=(
            jax.ShapeDtypeStruct((1, 1), jnp.int32),
            jax.ShapeDtypeStruct((n_chip, n_expert, 2 * CAP, width // n_chip), jnp.bfloat16),
            jax.ShapeDtypeStruct((CAP, tok_dev), jnp.bfloat16),
        ),
        in_specs=[smem, vmem, vmem, vmem, vmem],
        out_specs=(smem, vmem, vmem),
        cost_estimate=pl.CostEstimate(
            flops=4 * CAP * tok_dev * width, bytes_accessed=8 * tok_dev * width, transcendentals=0
        ),
        name="pick_rows",
    )(layout, routes.T, gates.T, tokens, cotangent)


def update_kernel(flags_ref, first_ref, second_ref, moved_ref, grad_ref, other_ref, new_first_ref, new_second_ref):
    rows = first_ref.shape[0]
    active = flags_ref[0] == 1
    base = pl.multiple_of(flags_ref[1] * rows, 16)
    step = 16
    for low in range(0, rows, step):
        span = slice(low, low + step)
        grad = grad_ref[pl.ds(base + low, step)] + other_ref[span].astype(jnp.float32)
        moved = moved_ref[span].astype(jnp.float32)
        kept = jnp.where(active, moved, first_ref[span])
        new_first_ref[span] = first_decay * kept + (1.0 - first_decay) * grad
        moved = moved_ref[rows + low : rows + low + step].astype(jnp.float32)
        kept = jnp.where(active, moved, second_ref[span])
        new_second_ref[span] = second_decay * kept + (1.0 - second_decay) * grad * grad


def update(active, core, first, second, mid, grad, other):
    vmem = pl.BlockSpec(memory_space=pltpu.VMEM)
    smem = pl.BlockSpec(memory_space=pltpu.SMEM)
    flags = jnp.stack((active.astype(jnp.int32), core))
    return pl.pallas_call(
        update_kernel,
        out_shape=(jax.ShapeDtypeStruct(first.shape, jnp.float32),) * 2,
        in_specs=[smem] + [vmem] * 5,
        out_specs=(vmem, vmem),
        cost_estimate=pl.CostEstimate(flops=8 * first.size, bytes_accessed=24 * first.size, transcendentals=0),
        name="update",
    )(flags, first, second, mid, grad, other)


def combine_kernel(pick_ref, returned_ref, after_ref, out_ref):
    n_chip, n_expert, cap, depth = returned_ref.shape
    pick = pick_ref[...]
    for chip in range(n_chip):
        rows = returned_ref[chip].astype(jnp.float32)
        total = jnp.sum(rows, axis=0).astype(jnp.bfloat16)
        spread = lax.dot_general(
            pick, total, (((0,), (0,)), ((), ())), preferred_element_type=jnp.float32
        )
        out_ref[:, chip * depth : (chip + 1) * depth] = spread.astype(jnp.bfloat16)


def combine(pick, returned, after):
    n_chip, n_expert, cap, depth = returned.shape
    tok_dev = pick.shape[1]
    vmem = pl.BlockSpec(memory_space=pltpu.VMEM)
    return pl.pallas_call(
        combine_kernel,
        out_shape=jax.ShapeDtypeStruct((tok_dev, n_chip * depth), jnp.bfloat16),
        in_specs=[vmem, vmem, pl.BlockSpec(memory_space=pl.ANY)],
        out_specs=vmem,
        cost_estimate=pl.CostEstimate(
            flops=2 * returned.size * tok_dev, bytes_accessed=4 * tok_dev * n_chip * depth, transcendentals=0
        ),
        name="combine",
    )(pick, returned, after)


def forward_backward(chip_weights, rows_in, grads_in):
    n_chip = lax.axis_size(CHIPS)
    width_dev = chip_weights.shape[1] // 3
    bf16 = jnp.bfloat16
    pre_part = jnp.dot(rows_in, chip_weights[:, : 2 * width_dev], preferred_element_type=jnp.float32)
    grad_part = jnp.dot(grads_in, chip_weights[:, 2 * width_dev :], preferred_element_type=jnp.float32)
    parts = jnp.concatenate((pre_part, grad_part), axis=1).astype(bf16)
    if n_chip > 4:
        sums = exchange(parts.reshape(n_chip, -1, parts.shape[1]), CHIPS)
        sums = jnp.sum(sums.astype(jnp.float32), axis=0).astype(bf16)
        sums = lax.all_gather(sums, CHIPS, axis=0, tiled=True).astype(jnp.float32)
    else:
        copies = jnp.broadcast_to(parts[None], (n_chip,) + parts.shape)
        sums = jnp.sum(exchange(copies, CHIPS).astype(jnp.float32), axis=0)
    gate_pre = sums[:, :width_dev]
    up_pre = sums[:, width_dev : 2 * width_dev]
    hidden_grad = sums[:, 2 * width_dev :]
    sigma = jax.nn.sigmoid(gate_pre)
    active_part = gate_pre * sigma
    hidden = active_part * up_pre
    gate_grad = hidden_grad * up_pre * sigma * (1.0 + gate_pre * (1.0 - sigma))
    up_grad = hidden_grad * active_part
    acts = jnp.concatenate((gate_grad, up_grad, hidden), axis=1).astype(bf16)
    part_rows = lax.dot_general(
        acts[:, : 2 * width_dev],
        chip_weights[:, : 2 * width_dev],
        (((1,), (1,)), ((), ())),
        preferred_element_type=jnp.float32,
    ).astype(bf16)
    return acts, part_rows


def weight_grads(rows_in, grads_in, acts, own_depth):
    width_dev = acts.shape[1] // 3
    across = (((0,), (0,)), ((), ()))
    proj_grad = lax.dot_general(
        rows_in, acts[:, : 2 * width_dev], across, preferred_element_type=jnp.float32
    )
    down_grad = lax.dot_general(
        grads_in, acts[:, 2 * width_dev :], across, preferred_element_type=jnp.float32
    )
    grad = jnp.concatenate((proj_grad, down_grad), axis=1)
    low, high = grad[:own_depth], grad[own_depth:]
    core = lax.axis_index("core")
    other = lax.ppermute(
        jnp.where(core == 0, high, low).astype(jnp.bfloat16), "core", [(0, 1), (1, 0)]
    )
    return grad, other


def send_back(part_rows):
    return exchange(part_rows.reshape(lax.axis_size(ACROSS), CAP, part_rows.shape[1]), ACROSS)


def add_up(returned, dest_token):
    n_chip, depth = lax.axis_size(CHIPS), returned.shape[-1]
    returned = returned.reshape(n_chip, -1, depth).transpose(1, 0, 2).reshape(-1, n_chip * depth)
    return lax.dot_general(
        dest_token, returned, (((0,), (0,)), ((), ())), preferred_element_type=jnp.float32
    ).astype(jnp.bfloat16)


def one_window(pair, sends, pick, weights, first_moment, second_moment):
    low, high = pair
    own_index = lax.axis_index("expert")
    active = (own_index == low) | (own_index == high)
    move = lambda block: lax.ppermute(block, "expert", [(low, high), (high, low)])
    bf16 = jnp.bfloat16
    first, second = first_moment[0], second_moment[0]
    depth = sends.shape[-1]

    block = jnp.where(active, move(weights[0]), weights[0])
    chip_weights = lax.all_gather(block, "core", axis=0, tiled=True)
    got = exchange(sends.reshape(-1, 2 * CAP, depth), ACROSS)
    moments = jnp.concatenate((first, second)).astype(bf16)
    got, moments = lax.optimization_barrier((got, moments))
    rows_in = got[:, :CAP].reshape(-1, depth)
    grads_in = got[:, CAP:].reshape(-1, depth)
    mid = move(moments)
    acts, part_rows = forward_backward(chip_weights, rows_in, grads_in)
    returned = send_back(part_rows)
    grad, other = weight_grads(rows_in, grads_in, acts, first.shape[0])
    new_first, new_second = update(
        active, lax.axis_index("core"), first, second, mid, grad, other
    )
    returned = returned.reshape(lax.axis_size(CHIPS), -1, CAP, depth)
    return combine(pick, returned, new_first), new_first[None], new_second[None]


def many_windows(tokens, cotangent, routes, gates, layout, weights, first_moment, second_moment):
    n_expert, n_chip = lax.axis_size("expert"), lax.axis_size(CHIPS)
    n_window = n_expert // HSPLIT
    own_index = lax.axis_index("expert")
    lane_ids = jnp.arange(n_expert, dtype=jnp.int32)
    placement, xor_mask, swap_on = layout[0], layout[1, 0], layout[2]
    held_slot = jnp.where(swap_on == 1, jnp.bitwise_xor(lane_ids, xor_mask), lane_ids)
    inverse = jnp.sum(
        jnp.where(placement[None, :] == lane_ids[:, None], lane_ids[None, :], 0), axis=1
    )
    slot_owner = inverse // HSPLIT
    expert_at = jnp.sum(
        jnp.where(held_slot[:, None] == lane_ids[None, :], slot_owner[None, :], 0), axis=1
    )
    active = select_lane(swap_on, lane_ids, own_index) == 1
    bf16 = jnp.bfloat16
    block = jnp.where(active, xor_rounds(weights[0], xor_mask), weights[0])
    moments = jnp.stack((first_moment[0], second_moment[0]))
    moved = xor_rounds(moments.astype(bf16), xor_mask).astype(jnp.float32)
    moments = jnp.where(active, moved, moments)

    tok_dev, top_count = routes.shape
    own_depth = weights.shape[1]
    depth = 2 * own_depth
    flat_ids = routes.reshape(-1)
    window_ids = jnp.arange(n_window, dtype=jnp.int32)
    hit_table = (flat_ids[:, None] == window_ids[None, :]).astype(jnp.int32)
    earlier = jnp.cumsum(hit_table, axis=0) - hit_table
    position = jnp.sum(earlier * hit_table, axis=1)
    kept = (flat_ids < n_window) & (position < CAP)
    slot_key = jnp.where(kept, flat_ids * CAP + position, -1)
    slot_pick = (jnp.arange(n_window * CAP, dtype=jnp.int32)[:, None] == slot_key[None, :]).astype(
        jnp.float32
    )
    assign_pick = slot_pick.reshape(n_window * CAP, tok_dev, top_count)
    slot_token = jnp.sum(assign_pick, axis=2)
    slot_gate = jnp.sum(assign_pick * gates[None], axis=(1, 2))[:, None]
    rows = jnp.dot(slot_token.astype(bf16), tokens, preferred_element_type=jnp.float32).astype(bf16)
    grads = jnp.dot(slot_token.astype(bf16), cotangent, preferred_element_type=jnp.float32)
    grads = (grads * slot_gate).astype(bf16)
    sends = jnp.stack((rows, grads)).reshape(2, n_window, CAP, n_chip, depth)
    sends = jnp.take(sends.transpose(3, 1, 0, 2, 4), expert_at, axis=1)
    dest_token = jnp.take(slot_token.reshape(n_window, CAP, tok_dev), expert_at, axis=0)
    dest_token = dest_token.reshape(n_expert * CAP, tok_dev).astype(bf16)
    got = exchange(sends.reshape(-1, 2 * CAP, depth), ACROSS)
    rows_in = got[:, :CAP].reshape(-1, depth)
    grads_in = got[:, CAP:].reshape(-1, depth)

    chip_weights = lax.all_gather(block, "core", axis=0, tiled=True)
    acts, part_rows = forward_backward(chip_weights, rows_in, grads_in)
    grad_input = add_up(send_back(part_rows), dest_token)
    grad, other = weight_grads(rows_in, grads_in, acts, own_depth)
    core = lax.axis_index("core")
    grad = jnp.where(core == 0, grad[:own_depth], grad[own_depth:]) + other.astype(jnp.float32)
    new_first = first_decay * moments[0] + (1.0 - first_decay) * grad
    new_second = second_decay * moments[1] + (1.0 - second_decay) * grad * grad
    return grad_input, new_first[None], new_second[None]


def local(tokens, cotangent, routes, gates, layout, weights, first_moment, second_moment):
    if lax.axis_size("expert") != HSPLIT:
        return many_windows(
            tokens, cotangent, routes, gates, layout, weights, first_moment, second_moment
        )
    case, sends, pick = pick_rows(layout, routes, gates, tokens, cotangent)
    branches = [functools.partial(one_window, pair) for pair in PAIRS]
    return lax.switch(case[0, 0], branches, sends, pick, weights, first_moment, second_moment)


def solution(mesh):
    n_dp, n_expert = mesh.devices.shape
    split = Mesh(mesh.devices.reshape(n_dp // 4, 2, 2, n_expert), ROWS)
    in_specs = (
        P(ROWS, None),
        P(ROWS, None),
        P(ROWS, None),
        P(ROWS, None),
        P(),
        P("expert", DP, None),
        P("expert", DP, None),
        P("expert", DP, None),
    )
    out_specs = (P(ROWS, None), P("expert", DP, None), P("expert", DP, None))
    return jax.shard_map(local, mesh=split, in_specs=in_specs, out_specs=out_specs, check_vma=False)
```

```python
import functools

import jax
import jax.numpy as jnp
from jax import lax
from jax.experimental import pallas as pl
from jax.experimental.pallas import tpu as pltpu
from jax.sharding import Mesh, PartitionSpec as P

HSPLIT = 4
CAP = 8


first_decay = 0.9
second_decay = 0.999

DP = ("outer", "inner", "core")
CHIPS = ("outer", "inner")
ROWS = DP + ("expert",)
ACROSS = CHIPS + ("expert",)
PAIRS = [(low, high) for low in range(4) for high in range(low + 1, 4)]
CUTS = (20, 30)


def xor_rounds(block, xor_mask):
    count = lax.axis_size("expert")
    for bit_pos in range(count.bit_length() - 1):
        route = [(lane, lane ^ (1 << bit_pos)) for lane in range(count)]
        partner_copy = lax.ppermute(block, "expert", route)
        flip_now = jnp.bitwise_and(jnp.right_shift(xor_mask, bit_pos), 1) == 1
        block = jnp.where(flip_now, partner_copy, block)
    return block


def select_lane(values, lane_ids, index_now):
    return jnp.sum(jnp.where(lane_ids == index_now, values, 0))


def exchange(block, axes):
    return lax.all_to_all(block, axes, split_axis=0, concat_axis=0, tiled=True)


def pick_kernel(layout_ref, routes_ref, gates_ref, tokens_ref, cot_ref, case_ref, sends_ref, pick_ref):
    n_chip, n_expert, _, depth = sends_ref.shape
    tok_dev = tokens_ref.shape[0]
    case_ref[0, 0] = layout_ref[2, 1] - layout_ref[2, 0] + 2 * layout_ref[2, 2] + 3 * layout_ref[2, 3]
    hit = jnp.where(routes_ref[...] == 0, 1.0, 0.0)
    gate = jnp.sum(hit * gates_ref[...], axis=0, keepdims=True)
    hit = jnp.broadcast_to(jnp.sum(hit, axis=0, keepdims=True), (CAP, tok_dev))
    row_ids = lax.broadcasted_iota(jnp.int32, (tok_dev, tok_dev), 0)
    col_ids = lax.broadcasted_iota(jnp.int32, (tok_dev, tok_dev), 1)
    before = jnp.where(row_ids < col_ids, 1.0, 0.0).astype(jnp.bfloat16)
    position = jnp.dot(hit.astype(jnp.bfloat16), before, preferred_element_type=jnp.float32)
    slots = lax.broadcasted_iota(jnp.int32, (CAP, tok_dev), 0).astype(jnp.float32)
    pick = jnp.where(position == slots, hit, 0.0)
    slot_gate = jnp.sum(pick * gate, axis=1, keepdims=True)
    pick = pick.astype(jnp.bfloat16)
    pick_ref[...] = pick
    for chip in range(n_chip):
        span = slice(chip * depth, (chip + 1) * depth)
        rows = jnp.dot(pick, tokens_ref[:, span], preferred_element_type=jnp.float32)
        grads = jnp.dot(pick, cot_ref[:, span], preferred_element_type=jnp.float32) * slot_gate
        both = jnp.concatenate((rows, grads), axis=0).astype(jnp.bfloat16)
        for expert in range(n_expert):
            sends_ref[chip, expert] = both


def pick_rows(layout, routes, gates, tokens, cotangent):
    tok_dev, width = tokens.shape
    n_chip, n_expert = lax.axis_size(CHIPS), lax.axis_size("expert")
    vmem = pl.BlockSpec(memory_space=pltpu.VMEM)
    smem = pl.BlockSpec(memory_space=pltpu.SMEM)
    return pl.pallas_call(
        pick_kernel,
        out_shape=(
            jax.ShapeDtypeStruct((1, 1), jnp.int32),
            jax.ShapeDtypeStruct((n_chip, n_expert, 2 * CAP, width // n_chip), jnp.bfloat16),
            jax.ShapeDtypeStruct((CAP, tok_dev), jnp.bfloat16),
        ),
        in_specs=[smem, vmem, vmem, vmem, vmem],
        out_specs=(smem, vmem, vmem),
        cost_estimate=pl.CostEstimate(
            flops=4 * CAP * tok_dev * width, bytes_accessed=8 * tok_dev * width, transcendentals=0
        ),
        name="pick_rows",
    )(layout, routes.T, gates.T, tokens, cotangent)


def update_kernel(flags_ref, first_ref, second_ref, moved_ref, grad_ref, other_ref, new_first_ref, new_second_ref):
    rows = first_ref.shape[0]
    active = flags_ref[0] == 1
    base = pl.multiple_of(flags_ref[1] * rows, 16)
    step = 16
    for low in range(0, rows, step):
        span = slice(low, low + step)
        grad = grad_ref[pl.ds(base + low, step)] + other_ref[span].astype(jnp.float32)
        moved = moved_ref[span].astype(jnp.float32)
        kept = jnp.where(active, moved, first_ref[span])
        new_first_ref[span] = first_decay * kept + (1.0 - first_decay) * grad
        moved = moved_ref[rows + low : rows + low + step].astype(jnp.float32)
        kept = jnp.where(active, moved, second_ref[span])
        new_second_ref[span] = second_decay * kept + (1.0 - second_decay) * grad * grad


def update(active, core, first, second, mid, grad, other):
    vmem = pl.BlockSpec(memory_space=pltpu.VMEM)
    smem = pl.BlockSpec(memory_space=pltpu.SMEM)
    flags = jnp.stack((active.astype(jnp.int32), core))
    return pl.pallas_call(
        update_kernel,
        out_shape=(jax.ShapeDtypeStruct(first.shape, jnp.float32),) * 2,
        in_specs=[smem] + [vmem] * 5,
        out_specs=(vmem, vmem),
        cost_estimate=pl.CostEstimate(flops=8 * first.size, bytes_accessed=24 * first.size, transcendentals=0),
        name="update",
    )(flags, first, second, mid, grad, other)


def combine_kernel(pick_ref, returned_ref, after_ref, out_ref):
    n_chip, n_expert, cap, depth = returned_ref.shape
    pick = pick_ref[...]
    for chip in range(n_chip):
        rows = returned_ref[chip].astype(jnp.float32)
        total = jnp.sum(rows, axis=0).astype(jnp.bfloat16)
        spread = lax.dot_general(
            pick, total, (((0,), (0,)), ((), ())), preferred_element_type=jnp.float32
        )
        out_ref[:, chip * depth : (chip + 1) * depth] = spread.astype(jnp.bfloat16)


def combine(pick, returned, after):
    n_chip, n_expert, cap, depth = returned.shape
    tok_dev = pick.shape[1]
    vmem = pl.BlockSpec(memory_space=pltpu.VMEM)
    return pl.pallas_call(
        combine_kernel,
        out_shape=jax.ShapeDtypeStruct((tok_dev, n_chip * depth), jnp.bfloat16),
        in_specs=[vmem, vmem, pl.BlockSpec(memory_space=pl.ANY)],
        out_specs=vmem,
        cost_estimate=pl.CostEstimate(
            flops=2 * returned.size * tok_dev, bytes_accessed=4 * tok_dev * n_chip * depth, transcendentals=0
        ),
        name="combine",
    )(pick, returned, after)


def forward_backward(chip_weights, rows_in, grads_in):
    n_chip = lax.axis_size(CHIPS)
    width_dev = chip_weights.shape[1] // 3
    bf16 = jnp.bfloat16
    pre_part = jnp.dot(rows_in, chip_weights[:, : 2 * width_dev], preferred_element_type=jnp.float32)
    grad_part = jnp.dot(grads_in, chip_weights[:, 2 * width_dev :], preferred_element_type=jnp.float32)
    parts = jnp.concatenate((pre_part, grad_part), axis=1).astype(bf16)
    if n_chip > 4:
        sums = exchange(parts.reshape(n_chip, -1, parts.shape[1]), CHIPS)
        sums = jnp.sum(sums.astype(jnp.float32), axis=0).astype(bf16)
        sums = lax.all_gather(sums, CHIPS, axis=0, tiled=True).astype(jnp.float32)
    else:
        sums = jnp.sum(lax.all_gather(parts, CHIPS, axis=0).astype(jnp.float32), axis=0)
    gate_pre = sums[:, :width_dev]
    up_pre = sums[:, width_dev : 2 * width_dev]
    hidden_grad = sums[:, 2 * width_dev :]
    sigma = jax.nn.sigmoid(gate_pre)
    active_part = gate_pre * sigma
    hidden = active_part * up_pre
    gate_grad = hidden_grad * up_pre * sigma * (1.0 + gate_pre * (1.0 - sigma))
    up_grad = hidden_grad * active_part
    acts = jnp.concatenate((gate_grad, up_grad, hidden), axis=1).astype(bf16)
    part_rows = lax.dot_general(
        acts[:, : 2 * width_dev],
        chip_weights[:, : 2 * width_dev],
        (((1,), (1,)), ((), ())),
        preferred_element_type=jnp.float32,
    ).astype(bf16)
    return acts, part_rows


def weight_grads(rows_in, grads_in, acts, own_depth):
    width_dev = acts.shape[1] // 3
    across = (((0,), (0,)), ((), ()))
    proj_grad = lax.dot_general(
        rows_in, acts[:, : 2 * width_dev], across, preferred_element_type=jnp.float32
    )
    down_grad = lax.dot_general(
        grads_in, acts[:, 2 * width_dev :], across, preferred_element_type=jnp.float32
    )
    grad = jnp.concatenate((proj_grad, down_grad), axis=1)
    low, high = grad[:own_depth], grad[own_depth:]
    core = lax.axis_index("core")
    other = lax.ppermute(
        jnp.where(core == 0, high, low).astype(jnp.bfloat16), "core", [(0, 1), (1, 0)]
    )
    return grad, other


def send_back(part_rows):
    return exchange(part_rows.reshape(lax.axis_size(ACROSS), CAP, part_rows.shape[1]), ACROSS)


def add_up(returned, dest_token):
    n_chip, depth = lax.axis_size(CHIPS), returned.shape[-1]
    returned = returned.reshape(n_chip, -1, depth).transpose(1, 0, 2).reshape(-1, n_chip * depth)
    return lax.dot_general(
        dest_token, returned, (((0,), (0,)), ((), ())), preferred_element_type=jnp.float32
    ).astype(jnp.bfloat16)


def one_window(pair, valid, sends, pick, weights, first_moment, second_moment):
    low, high = pair
    own_index = lax.axis_index("expert")
    active = (own_index == low) | (own_index == high)
    move = lambda block: lax.ppermute(block, "expert", [(low, high), (high, low)])
    bf16 = jnp.bfloat16
    first, second = first_moment[0], second_moment[0]
    depth = sends.shape[-1]

    block = jnp.where(active, move(weights[0]), weights[0])
    chip_weights = lax.all_gather(block, "core", axis=0, tiled=True)
    got = exchange(sends.reshape(-1, 2 * CAP, depth), ACROSS)
    moments = jnp.concatenate((first, second)).astype(bf16)
    got, moments = lax.optimization_barrier((got, moments))
    rows_in = got[:, :CAP].reshape(-1, depth)
    grads_in = got[:, CAP:].reshape(-1, depth)
    mid = move(moments)
    shapes = jax.eval_shape(forward_backward, chip_weights, rows_in, grads_in)
    acts, part_rows = lax.cond(
        valid,
        forward_backward,
        lambda *_: tuple(jnp.zeros(shape.shape, shape.dtype) for shape in shapes),
        chip_weights,
        rows_in,
        grads_in,
    )
    returned = send_back(part_rows)
    grad, other = weight_grads(rows_in, grads_in, acts, first.shape[0])
    new_first, new_second = update(
        active, lax.axis_index("core"), first, second, mid, grad, other
    )
    returned = returned.reshape(lax.axis_size(CHIPS), -1, CAP, depth)
    return combine(pick, returned, new_first), new_first[None], new_second[None]


def many_windows(tokens, cotangent, routes, gates, layout, weights, first_moment, second_moment):
    n_expert, n_chip = lax.axis_size("expert"), lax.axis_size(CHIPS)
    n_window = n_expert // HSPLIT
    own_index = lax.axis_index("expert")
    lane_ids = jnp.arange(n_expert, dtype=jnp.int32)
    placement, xor_mask, swap_on = layout[0], layout[1, 0], layout[2]
    held_slot = jnp.where(swap_on == 1, jnp.bitwise_xor(lane_ids, xor_mask), lane_ids)
    inverse = jnp.sum(
        jnp.where(placement[None, :] == lane_ids[:, None], lane_ids[None, :], 0), axis=1
    )
    slot_owner = inverse // HSPLIT
    expert_at = jnp.sum(
        jnp.where(held_slot[:, None] == lane_ids[None, :], slot_owner[None, :], 0), axis=1
    )
    active = select_lane(swap_on, lane_ids, own_index) == 1
    bf16 = jnp.bfloat16
    block = jnp.where(active, xor_rounds(weights[0], xor_mask), weights[0])
    moments = jnp.stack((first_moment[0], second_moment[0]))
    moved = xor_rounds(moments.astype(bf16), xor_mask).astype(jnp.float32)
    moments = jnp.where(active, moved, moments)

    tok_dev, top_count = routes.shape
    own_depth = weights.shape[1]
    depth = 2 * own_depth
    flat_ids = routes.reshape(-1)
    window_ids = jnp.arange(n_window, dtype=jnp.int32)
    hit_table = (flat_ids[:, None] == window_ids[None, :]).astype(jnp.int32)
    earlier = jnp.cumsum(hit_table, axis=0) - hit_table
    position = jnp.sum(earlier * hit_table, axis=1)
    kept = (flat_ids < n_window) & (position < CAP)
    slot_key = jnp.where(kept, flat_ids * CAP + position, -1)
    slot_pick = (jnp.arange(n_window * CAP, dtype=jnp.int32)[:, None] == slot_key[None, :]).astype(
        jnp.float32
    )
    assign_pick = slot_pick.reshape(n_window * CAP, tok_dev, top_count)
    slot_token = jnp.sum(assign_pick, axis=2)
    slot_gate = jnp.sum(assign_pick * gates[None], axis=(1, 2))[:, None]
    rows = jnp.dot(slot_token.astype(bf16), tokens, preferred_element_type=jnp.float32).astype(bf16)
    grads = jnp.dot(slot_token.astype(bf16), cotangent, preferred_element_type=jnp.float32)
    grads = (grads * slot_gate).astype(bf16)
    sends = jnp.stack((rows, grads)).reshape(2, n_window, CAP, n_chip, depth)
    sends = jnp.take(sends.transpose(3, 1, 0, 2, 4), expert_at, axis=1)
    dest_token = jnp.take(slot_token.reshape(n_window, CAP, tok_dev), expert_at, axis=0)
    dest_token = dest_token.reshape(n_expert * CAP, tok_dev).astype(bf16)
    got = exchange(sends.reshape(-1, 2 * CAP, depth), ACROSS)
    rows_in = got[:, :CAP].reshape(-1, depth)
    grads_in = got[:, CAP:].reshape(-1, depth)

    chip_weights = lax.all_gather(block, "core", axis=0, tiled=True)
    acts, part_rows = forward_backward(chip_weights, rows_in, grads_in)
    grad_input = add_up(send_back(part_rows), dest_token)
    grad, other = weight_grads(rows_in, grads_in, acts, own_depth)
    core = lax.axis_index("core")
    grad = jnp.where(core == 0, grad[:own_depth], grad[own_depth:]) + other.astype(jnp.float32)
    new_first = first_decay * moments[0] + (1.0 - first_decay) * grad
    new_second = second_decay * moments[1] + (1.0 - second_decay) * grad * grad
    return grad_input, new_first[None], new_second[None]


def local(tokens, cotangent, routes, gates, layout, weights, first_moment, second_moment):
    if lax.axis_size("expert") != HSPLIT:
        return many_windows(
            tokens, cotangent, routes, gates, layout, weights, first_moment, second_moment
        )
    case, sends, pick = pick_rows(layout, routes, gates, tokens, cotangent)
    branches = [functools.partial(one_window, pair) for pair in PAIRS]
    case = case[0, 0]
    return lax.switch(case, branches, case >= 0, sends, pick, weights, first_moment, second_moment)


def solution(mesh):
    n_dp, n_expert = mesh.devices.shape
    split = Mesh(mesh.devices.reshape(n_dp // 4, 2, 2, n_expert), ROWS)
    in_specs = (
        P(ROWS, None),
        P(ROWS, None),
        P(ROWS, None),
        P(ROWS, None),
        P(),
        P("expert", DP, None),
        P("expert", DP, None),
        P("expert", DP, None),
    )
    out_specs = (P(ROWS, None), P("expert", DP, None), P("expert", DP, None))
    return jax.shard_map(local, mesh=split, in_specs=in_specs, out_specs=out_specs, check_vma=False)
```

```python
import functools

import jax
import jax.numpy as jnp
from jax import lax
from jax.experimental import pallas as pl
from jax.experimental.pallas import tpu as pltpu
from jax.sharding import Mesh, PartitionSpec as P

HSPLIT = 4
CAP = 8


first_decay = 0.9
second_decay = 0.999

DP = ("outer", "inner", "core")
CHIPS = ("outer", "inner")
ROWS = DP + ("expert",)
ACROSS = CHIPS + ("expert",)
PAIRS = [(low, high) for low in range(4) for high in range(low + 1, 4)]
CUTS = (20, 30)


def xor_rounds(block, xor_mask):
    count = lax.axis_size("expert")
    for bit_pos in range(count.bit_length() - 1):
        route = [(lane, lane ^ (1 << bit_pos)) for lane in range(count)]
        partner_copy = lax.ppermute(block, "expert", route)
        flip_now = jnp.bitwise_and(jnp.right_shift(xor_mask, bit_pos), 1) == 1
        block = jnp.where(flip_now, partner_copy, block)
    return block


def select_lane(values, lane_ids, index_now):
    return jnp.sum(jnp.where(lane_ids == index_now, values, 0))


def exchange(block, axes):
    return lax.all_to_all(block, axes, split_axis=0, concat_axis=0, tiled=True)


def case_kernel(layout_ref, case_ref):
    case_ref[0, 0] = layout_ref[2, 1] - layout_ref[2, 0] + 2 * layout_ref[2, 2] + 3 * layout_ref[2, 3]


def swapping_pair(layout):
    smem = pl.BlockSpec(memory_space=pltpu.SMEM)
    return pl.pallas_call(
        case_kernel,
        out_shape=jax.ShapeDtypeStruct((1, 1), jnp.int32),
        in_specs=[smem],
        out_specs=smem,
        name="swapping_pair",
    )(layout)[0, 0]


def pick_kernel(routes_ref, gates_ref, tokens_ref, cot_ref, sends_ref, pick_ref):
    n_chip, n_expert, _, depth = sends_ref.shape
    tok_dev = tokens_ref.shape[0]
    hit = jnp.where(routes_ref[...] == 0, 1.0, 0.0)
    gate = jnp.sum(hit * gates_ref[...], axis=0, keepdims=True)
    hit = jnp.broadcast_to(jnp.sum(hit, axis=0, keepdims=True), (CAP, tok_dev))
    row_ids = lax.broadcasted_iota(jnp.int32, (tok_dev, tok_dev), 0)
    col_ids = lax.broadcasted_iota(jnp.int32, (tok_dev, tok_dev), 1)
    before = jnp.where(row_ids < col_ids, 1.0, 0.0).astype(jnp.bfloat16)
    position = jnp.dot(hit.astype(jnp.bfloat16), before, preferred_element_type=jnp.float32)
    slots = lax.broadcasted_iota(jnp.int32, (CAP, tok_dev), 0).astype(jnp.float32)
    pick = jnp.where(position == slots, hit, 0.0)
    slot_gate = jnp.sum(pick * gate, axis=1, keepdims=True)
    pick_ref[...] = jnp.concatenate((pick,) * n_expert, axis=0).T.astype(jnp.bfloat16)
    pick = pick.astype(jnp.bfloat16)
    for chip in range(n_chip):
        span = slice(chip * depth, (chip + 1) * depth)
        rows = jnp.dot(pick, tokens_ref[:, span], preferred_element_type=jnp.float32)
        grads = jnp.dot(pick, cot_ref[:, span], preferred_element_type=jnp.float32) * slot_gate
        both = jnp.concatenate((rows, grads), axis=0).astype(jnp.bfloat16)
        for expert in range(n_expert):
            sends_ref[chip, expert] = both


def pick_rows(routes, gates, tokens, cotangent):
    tok_dev, width = tokens.shape
    n_chip, n_expert = lax.axis_size(CHIPS), lax.axis_size("expert")
    vmem = pl.BlockSpec(memory_space=pltpu.VMEM)
    return pl.pallas_call(
        pick_kernel,
        out_shape=(
            jax.ShapeDtypeStruct((n_chip, n_expert, 2 * CAP, width // n_chip), jnp.bfloat16),
            jax.ShapeDtypeStruct((tok_dev, n_expert * CAP), jnp.bfloat16),
        ),
        in_specs=[vmem] * 4,
        out_specs=(vmem, vmem),
        cost_estimate=pl.CostEstimate(
            flops=4 * CAP * tok_dev * width, bytes_accessed=8 * tok_dev * width, transcendentals=0
        ),
        name="pick_rows",
    )(routes.T, gates.T, tokens, cotangent)


def update_kernel(flags_ref, first_ref, second_ref, moved_ref, grad_ref, other_ref, new_first_ref, new_second_ref):
    rows = first_ref.shape[0]
    active = flags_ref[0] == 1
    base = pl.multiple_of(flags_ref[1] * rows, 16)
    step = 16
    for low in range(0, rows, step):
        span = slice(low, low + step)
        grad = grad_ref[pl.ds(base + low, step)] + other_ref[span].astype(jnp.float32)
        moved = moved_ref[span].astype(jnp.float32)
        kept = jnp.where(active, moved, first_ref[span])
        new_first_ref[span] = first_decay * kept + (1.0 - first_decay) * grad
        moved = moved_ref[rows + low : rows + low + step].astype(jnp.float32)
        kept = jnp.where(active, moved, second_ref[span])
        new_second_ref[span] = second_decay * kept + (1.0 - second_decay) * grad * grad


def update(active, core, first, second, mid, grad, other):
    vmem = pl.BlockSpec(memory_space=pltpu.VMEM)
    smem = pl.BlockSpec(memory_space=pltpu.SMEM)
    flags = jnp.stack((active.astype(jnp.int32), core))
    return pl.pallas_call(
        update_kernel,
        out_shape=(jax.ShapeDtypeStruct(first.shape, jnp.float32),) * 2,
        in_specs=[smem] + [vmem] * 5,
        out_specs=(vmem, vmem),
        cost_estimate=pl.CostEstimate(flops=8 * first.size, bytes_accessed=24 * first.size, transcendentals=0),
        name="update",
    )(flags, first, second, mid, grad, other)


def combine_kernel(pick_ref, returned_ref, first_ref, out_ref):
    slots = pick_ref.shape[1]
    depth = returned_ref.shape[1]
    for chip in range(returned_ref.shape[0] // slots):
        rows = returned_ref[chip * slots : (chip + 1) * slots]
        out_ref[:, chip * depth : (chip + 1) * depth] = jnp.dot(
            pick_ref[...], rows, preferred_element_type=jnp.float32
        ).astype(jnp.bfloat16)


def combine(pick, returned, first):
    tok_dev, slots = pick.shape
    rows, depth = returned.shape
    width = rows // slots * depth
    vmem, hbm = pl.BlockSpec(memory_space=pltpu.VMEM), pl.BlockSpec(memory_space=pl.ANY)
    return pl.pallas_call(
        combine_kernel,
        out_shape=jax.ShapeDtypeStruct((tok_dev, width), jnp.bfloat16),
        in_specs=[vmem, vmem, hbm],
        out_specs=vmem,
        cost_estimate=pl.CostEstimate(
            flops=2 * returned.size * tok_dev, bytes_accessed=4 * tok_dev * width, transcendentals=0
        ),
        name="combine",
    )(pick, returned, first)


def forward_backward(chip_weights, rows_in, grads_in):
    n_chip = lax.axis_size(CHIPS)
    width_dev = chip_weights.shape[1] // 3
    bf16 = jnp.bfloat16
    pre_part = jnp.dot(rows_in, chip_weights[:, : 2 * width_dev], preferred_element_type=jnp.float32)
    grad_part = jnp.dot(grads_in, chip_weights[:, 2 * width_dev :], preferred_element_type=jnp.float32)
    parts = jnp.concatenate((pre_part, grad_part), axis=1).astype(bf16)
    if n_chip > 4:
        sums = exchange(parts.reshape(n_chip, -1, parts.shape[1]), CHIPS)
        sums = jnp.sum(sums.astype(jnp.float32), axis=0).astype(bf16)
        sums = lax.all_gather(sums, CHIPS, axis=0, tiled=True).astype(jnp.float32)
    else:
        sums = jnp.sum(lax.all_gather(parts, CHIPS, axis=0).astype(jnp.float32), axis=0)
    gate_pre = sums[:, :width_dev]
    up_pre = sums[:, width_dev : 2 * width_dev]
    hidden_grad = sums[:, 2 * width_dev :]
    sigma = jax.nn.sigmoid(gate_pre)
    active_part = gate_pre * sigma
    hidden = active_part * up_pre
    gate_grad = hidden_grad * up_pre * sigma * (1.0 + gate_pre * (1.0 - sigma))
    up_grad = hidden_grad * active_part
    acts = jnp.concatenate((gate_grad, up_grad, hidden), axis=1).astype(bf16)
    part_rows = lax.dot_general(
        acts[:, : 2 * width_dev],
        chip_weights[:, : 2 * width_dev],
        (((1,), (1,)), ((), ())),
        preferred_element_type=jnp.float32,
    ).astype(bf16)
    return acts, part_rows


def weight_grads(rows_in, grads_in, acts, own_depth):
    width_dev = acts.shape[1] // 3
    across = (((0,), (0,)), ((), ()))
    proj_grad = lax.dot_general(
        rows_in, acts[:, : 2 * width_dev], across, preferred_element_type=jnp.float32
    )
    down_grad = lax.dot_general(
        grads_in, acts[:, 2 * width_dev :], across, preferred_element_type=jnp.float32
    )
    grad = jnp.concatenate((proj_grad, down_grad), axis=1)
    low, high = grad[:own_depth], grad[own_depth:]
    core = lax.axis_index("core")
    other = lax.ppermute(
        jnp.where(core == 0, high, low).astype(jnp.bfloat16), "core", [(0, 1), (1, 0)]
    )
    return grad, other


def send_back(part_rows):
    return exchange(part_rows.reshape(lax.axis_size(ACROSS), CAP, part_rows.shape[1]), ACROSS)


def add_up(returned, dest_token):
    n_chip, depth = lax.axis_size(CHIPS), returned.shape[-1]
    returned = returned.reshape(n_chip, -1, depth).transpose(1, 0, 2).reshape(-1, n_chip * depth)
    return lax.dot_general(
        dest_token, returned, (((0,), (0,)), ((), ())), preferred_element_type=jnp.float32
    ).astype(jnp.bfloat16)


def one_window(pair, case, routes, gates, tokens, cotangent, weights, first_moment, second_moment):
    low, high = pair
    own_index = lax.axis_index("expert")
    active = (own_index == low) | (own_index == high)
    move = lambda block: lax.ppermute(block, "expert", [(low, high), (high, low)])
    bf16 = jnp.bfloat16
    first, second = first_moment[0], second_moment[0]
    depth = 2 * first.shape[0]

    block = jnp.where(active, move(weights[0]), weights[0])
    chip_weights = lax.all_gather(block, "core", axis=0, tiled=True)
    sends, pick = pick_rows(routes, gates, tokens, cotangent)
    got = exchange(sends.reshape(-1, 2 * CAP, depth), ACROSS)
    moments = jnp.concatenate((first, second)).astype(bf16)
    chip_weights, moments = lax.optimization_barrier((chip_weights, moments))
    rows_in = got[:, :CAP].reshape(-1, depth)
    grads_in = got[:, CAP:].reshape(-1, depth)
    mid = move(moments)
    shapes = jax.eval_shape(forward_backward, chip_weights, rows_in, grads_in)
    acts, part_rows = lax.cond(
        case >= 0,
        forward_backward,
        lambda *_: tuple(jnp.zeros(shape.shape, shape.dtype) for shape in shapes),
        chip_weights,
        rows_in,
        grads_in,
    )
    returned = send_back(part_rows)
    grad, other = weight_grads(rows_in, grads_in, acts, first.shape[0])
    new_first, new_second = update(
        active, lax.axis_index("core"), first, second, mid, grad, other
    )
    returned = returned.reshape(-1, depth)
    return combine(pick, returned, new_first), new_first[None], new_second[None]


def many_windows(tokens, cotangent, routes, gates, layout, weights, first_moment, second_moment):
    n_expert, n_chip = lax.axis_size("expert"), lax.axis_size(CHIPS)
    n_window = n_expert // HSPLIT
    own_index = lax.axis_index("expert")
    lane_ids = jnp.arange(n_expert, dtype=jnp.int32)
    placement, xor_mask, swap_on = layout[0], layout[1, 0], layout[2]
    held_slot = jnp.where(swap_on == 1, jnp.bitwise_xor(lane_ids, xor_mask), lane_ids)
    inverse = jnp.sum(
        jnp.where(placement[None, :] == lane_ids[:, None], lane_ids[None, :], 0), axis=1
    )
    slot_owner = inverse // HSPLIT
    expert_at = jnp.sum(
        jnp.where(held_slot[:, None] == lane_ids[None, :], slot_owner[None, :], 0), axis=1
    )
    active = select_lane(swap_on, lane_ids, own_index) == 1
    bf16 = jnp.bfloat16
    block = jnp.where(active, xor_rounds(weights[0], xor_mask), weights[0])
    moments = jnp.stack((first_moment[0], second_moment[0]))
    moved = xor_rounds(moments.astype(bf16), xor_mask).astype(jnp.float32)
    moments = jnp.where(active, moved, moments)

    tok_dev, top_count = routes.shape
    own_depth = weights.shape[1]
    depth = 2 * own_depth
    flat_ids = routes.reshape(-1)
    window_ids = jnp.arange(n_window, dtype=jnp.int32)
    hit_table = (flat_ids[:, None] == window_ids[None, :]).astype(jnp.int32)
    earlier = jnp.cumsum(hit_table, axis=0) - hit_table
    position = jnp.sum(earlier * hit_table, axis=1)
    kept = (flat_ids < n_window) & (position < CAP)
    slot_key = jnp.where(kept, flat_ids * CAP + position, -1)
    slot_pick = (jnp.arange(n_window * CAP, dtype=jnp.int32)[:, None] == slot_key[None, :]).astype(
        jnp.float32
    )
    assign_pick = slot_pick.reshape(n_window * CAP, tok_dev, top_count)
    slot_token = jnp.sum(assign_pick, axis=2)
    slot_gate = jnp.sum(assign_pick * gates[None], axis=(1, 2))[:, None]
    rows = jnp.dot(slot_token.astype(bf16), tokens, preferred_element_type=jnp.float32).astype(bf16)
    grads = jnp.dot(slot_token.astype(bf16), cotangent, preferred_element_type=jnp.float32)
    grads = (grads * slot_gate).astype(bf16)
    sends = jnp.stack((rows, grads)).reshape(2, n_window, CAP, n_chip, depth)
    sends = jnp.take(sends.transpose(3, 1, 0, 2, 4), expert_at, axis=1)
    dest_token = jnp.take(slot_token.reshape(n_window, CAP, tok_dev), expert_at, axis=0)
    dest_token = dest_token.reshape(n_expert * CAP, tok_dev).astype(bf16)
    got = exchange(sends.reshape(-1, 2 * CAP, depth), ACROSS)
    rows_in = got[:, :CAP].reshape(-1, depth)
    grads_in = got[:, CAP:].reshape(-1, depth)

    chip_weights = lax.all_gather(block, "core", axis=0, tiled=True)
    acts, part_rows = forward_backward(chip_weights, rows_in, grads_in)
    grad_input = add_up(send_back(part_rows), dest_token)
    grad, other = weight_grads(rows_in, grads_in, acts, own_depth)
    core = lax.axis_index("core")
    grad = jnp.where(core == 0, grad[:own_depth], grad[own_depth:]) + other.astype(jnp.float32)
    new_first = first_decay * moments[0] + (1.0 - first_decay) * grad
    new_second = second_decay * moments[1] + (1.0 - second_decay) * grad * grad
    return grad_input, new_first[None], new_second[None]


def local(tokens, cotangent, routes, gates, layout, weights, first_moment, second_moment):
    if lax.axis_size("expert") != HSPLIT:
        return many_windows(
            tokens, cotangent, routes, gates, layout, weights, first_moment, second_moment
        )
    case = swapping_pair(layout)
    branches = [functools.partial(one_window, pair) for pair in PAIRS]
    return lax.switch(
        case, branches, case, routes, gates, tokens, cotangent, weights, first_moment, second_moment
    )


def solution(mesh):
    n_dp, n_expert = mesh.devices.shape
    split = Mesh(mesh.devices.reshape(n_dp // 4, 2, 2, n_expert), ROWS)
    in_specs = (
        P(ROWS, None),
        P(ROWS, None),
        P(ROWS, None),
        P(ROWS, None),
        P(),
        P("expert", DP, None),
        P("expert", DP, None),
        P("expert", DP, None),
    )
    out_specs = (P(ROWS, None), P("expert", DP, None), P("expert", DP, None))
    return jax.shard_map(local, mesh=split, in_specs=in_specs, out_specs=out_specs, check_vma=False)
```

```python
import functools

import jax
import jax.numpy as jnp
from jax import lax
from jax.experimental import pallas as pl
from jax.experimental.pallas import tpu as pltpu
from jax.sharding import Mesh, PartitionSpec as P

HSPLIT = 4
CAP = 8


first_decay = 0.9
second_decay = 0.999

DP = ("outer", "inner", "core")
CHIPS = ("outer", "inner")
ROWS = DP + ("expert",)
ACROSS = CHIPS + ("expert",)
PAIRS = [(low, high) for low in range(4) for high in range(low + 1, 4)]
CUTS = (20, 30)


def xor_rounds(block, xor_mask):
    count = lax.axis_size("expert")
    for bit_pos in range(count.bit_length() - 1):
        route = [(lane, lane ^ (1 << bit_pos)) for lane in range(count)]
        partner_copy = lax.ppermute(block, "expert", route)
        flip_now = jnp.bitwise_and(jnp.right_shift(xor_mask, bit_pos), 1) == 1
        block = jnp.where(flip_now, partner_copy, block)
    return block


def select_lane(values, lane_ids, index_now):
    return jnp.sum(jnp.where(lane_ids == index_now, values, 0))


def exchange(block, axes):
    return lax.all_to_all(block, axes, split_axis=0, concat_axis=0, tiled=True)


def case_kernel(layout_ref, case_ref):
    case_ref[0, 0] = layout_ref[2, 1] - layout_ref[2, 0] + 2 * layout_ref[2, 2] + 3 * layout_ref[2, 3]


def swapping_pair(layout):
    smem = pl.BlockSpec(memory_space=pltpu.SMEM)
    return pl.pallas_call(
        case_kernel,
        out_shape=jax.ShapeDtypeStruct((1, 1), jnp.int32),
        in_specs=[smem],
        out_specs=smem,
        name="swapping_pair",
    )(layout)[0, 0]


def pick_kernel(routes_ref, gates_ref, tokens_ref, cot_ref, sends_ref, pick_ref):
    n_chip, n_expert, _, depth = sends_ref.shape
    tok_dev = tokens_ref.shape[0]
    hit = jnp.where(routes_ref[...] == 0, 1.0, 0.0)
    gate = jnp.sum(hit * gates_ref[...], axis=0, keepdims=True)
    hit = jnp.broadcast_to(jnp.sum(hit, axis=0, keepdims=True), (CAP, tok_dev))
    row_ids = lax.broadcasted_iota(jnp.int32, (tok_dev, tok_dev), 0)
    col_ids = lax.broadcasted_iota(jnp.int32, (tok_dev, tok_dev), 1)
    before = jnp.where(row_ids < col_ids, 1.0, 0.0).astype(jnp.bfloat16)
    position = jnp.dot(hit.astype(jnp.bfloat16), before, preferred_element_type=jnp.float32)
    slots = lax.broadcasted_iota(jnp.int32, (CAP, tok_dev), 0).astype(jnp.float32)
    pick = jnp.where(position == slots, hit, 0.0)
    slot_gate = jnp.sum(pick * gate, axis=1, keepdims=True)
    pick_ref[...] = jnp.concatenate((pick,) * n_expert, axis=0).T.astype(jnp.bfloat16)
    pick = pick.astype(jnp.bfloat16)
    for chip in range(n_chip):
        span = slice(chip * depth, (chip + 1) * depth)
        rows = jnp.dot(pick, tokens_ref[:, span], preferred_element_type=jnp.float32)
        grads = jnp.dot(pick, cot_ref[:, span], preferred_element_type=jnp.float32) * slot_gate
        both = jnp.concatenate((rows, grads), axis=0).astype(jnp.bfloat16)
        for expert in range(n_expert):
            sends_ref[chip, expert] = both


def pick_rows(routes, gates, tokens, cotangent):
    tok_dev, width = tokens.shape
    n_chip, n_expert = lax.axis_size(CHIPS), lax.axis_size("expert")
    vmem = pl.BlockSpec(memory_space=pltpu.VMEM)
    return pl.pallas_call(
        pick_kernel,
        out_shape=(
            jax.ShapeDtypeStruct((n_chip, n_expert, 2 * CAP, width // n_chip), jnp.bfloat16),
            jax.ShapeDtypeStruct((tok_dev, n_expert * CAP), jnp.bfloat16),
        ),
        in_specs=[vmem] * 4,
        out_specs=(vmem, vmem),
        cost_estimate=pl.CostEstimate(
            flops=4 * CAP * tok_dev * width, bytes_accessed=8 * tok_dev * width, transcendentals=0
        ),
        name="pick_rows",
    )(routes.T, gates.T, tokens, cotangent)


def update_kernel(flags_ref, first_ref, second_ref, moved_ref, grad_ref, other_ref, new_first_ref, new_second_ref):
    rows = first_ref.shape[0]
    active = flags_ref[0] == 1
    base = pl.multiple_of(flags_ref[1] * rows, 16)
    step = 16
    for low in range(0, rows, step):
        span = slice(low, low + step)
        grad = grad_ref[pl.ds(base + low, step)] + other_ref[span].astype(jnp.float32)
        moved = moved_ref[span].astype(jnp.float32)
        kept = jnp.where(active, moved, first_ref[span])
        new_first_ref[span] = first_decay * kept + (1.0 - first_decay) * grad
        moved = moved_ref[rows + low : rows + low + step].astype(jnp.float32)
        kept = jnp.where(active, moved, second_ref[span])
        new_second_ref[span] = second_decay * kept + (1.0 - second_decay) * grad * grad


def update(active, core, first, second, mid, grad, other):
    vmem = pl.BlockSpec(memory_space=pltpu.VMEM)
    smem = pl.BlockSpec(memory_space=pltpu.SMEM)
    flags = jnp.stack((active.astype(jnp.int32), core))
    return pl.pallas_call(
        update_kernel,
        out_shape=(jax.ShapeDtypeStruct(first.shape, jnp.float32),) * 2,
        in_specs=[smem] + [vmem] * 5,
        out_specs=(vmem, vmem),
        cost_estimate=pl.CostEstimate(flops=8 * first.size, bytes_accessed=24 * first.size, transcendentals=0),
        compiler_params=pltpu.CompilerParams(vmem_limit_bytes=12 << 20),
        name="update",
    )(flags, first, second, mid, grad, other)


def combine_kernel(pick_ref, returned_ref, first_ref, out_ref):
    slots = pick_ref.shape[1]
    depth = returned_ref.shape[1]
    for chip in range(returned_ref.shape[0] // slots):
        rows = returned_ref[chip * slots : (chip + 1) * slots]
        out_ref[:, chip * depth : (chip + 1) * depth] = jnp.dot(
            pick_ref[...], rows, preferred_element_type=jnp.float32
        ).astype(jnp.bfloat16)


def combine(pick, returned, first):
    tok_dev, slots = pick.shape
    rows, depth = returned.shape
    width = rows // slots * depth
    vmem, hbm = pl.BlockSpec(memory_space=pltpu.VMEM), pl.BlockSpec(memory_space=pl.ANY)
    return pl.pallas_call(
        combine_kernel,
        out_shape=jax.ShapeDtypeStruct((tok_dev, width), jnp.bfloat16),
        in_specs=[vmem, vmem, hbm],
        out_specs=vmem,
        cost_estimate=pl.CostEstimate(
            flops=2 * returned.size * tok_dev, bytes_accessed=4 * tok_dev * width, transcendentals=0
        ),
        compiler_params=pltpu.CompilerParams(vmem_limit_bytes=4 << 20),
        name="combine",
    )(pick, returned, first)


def forward_backward(chip_weights, rows_in, grads_in):
    n_chip = lax.axis_size(CHIPS)
    width_dev = chip_weights.shape[1] // 3
    bf16 = jnp.bfloat16
    pre_part = jnp.dot(rows_in, chip_weights[:, : 2 * width_dev], preferred_element_type=jnp.float32)
    grad_part = jnp.dot(grads_in, chip_weights[:, 2 * width_dev :], preferred_element_type=jnp.float32)
    parts = jnp.concatenate((pre_part, grad_part), axis=1).astype(bf16)
    if n_chip > 4:
        sums = exchange(parts.reshape(n_chip, -1, parts.shape[1]), CHIPS)
        sums = jnp.sum(sums.astype(jnp.float32), axis=0).astype(bf16)
        sums = lax.all_gather(sums, CHIPS, axis=0, tiled=True).astype(jnp.float32)
    else:
        sums = jnp.sum(lax.all_gather(parts, CHIPS, axis=0).astype(jnp.float32), axis=0)
    gate_pre = sums[:, :width_dev]
    up_pre = sums[:, width_dev : 2 * width_dev]
    hidden_grad = sums[:, 2 * width_dev :]
    sigma = jax.nn.sigmoid(gate_pre)
    active_part = gate_pre * sigma
    hidden = active_part * up_pre
    gate_grad = hidden_grad * up_pre * sigma * (1.0 + gate_pre * (1.0 - sigma))
    up_grad = hidden_grad * active_part
    acts = jnp.concatenate((gate_grad, up_grad, hidden), axis=1).astype(bf16)
    part_rows = lax.dot_general(
        acts[:, : 2 * width_dev],
        chip_weights[:, : 2 * width_dev],
        (((1,), (1,)), ((), ())),
        preferred_element_type=jnp.float32,
    ).astype(bf16)
    return acts, part_rows


def weight_grads(rows_in, grads_in, acts, own_depth):
    width_dev = acts.shape[1] // 3
    across = (((0,), (0,)), ((), ()))
    proj_grad = lax.dot_general(
        rows_in, acts[:, : 2 * width_dev], across, preferred_element_type=jnp.float32
    )
    down_grad = lax.dot_general(
        grads_in, acts[:, 2 * width_dev :], across, preferred_element_type=jnp.float32
    )
    grad = jnp.concatenate((proj_grad, down_grad), axis=1)
    low, high = grad[:own_depth], grad[own_depth:]
    core = lax.axis_index("core")
    other = lax.ppermute(
        jnp.where(core == 0, high, low).astype(jnp.bfloat16), "core", [(0, 1), (1, 0)]
    )
    return grad, other


def send_back(part_rows):
    return exchange(part_rows.reshape(lax.axis_size(ACROSS), CAP, part_rows.shape[1]), ACROSS)


def add_up(returned, dest_token):
    n_chip, depth = lax.axis_size(CHIPS), returned.shape[-1]
    returned = returned.reshape(n_chip, -1, depth).transpose(1, 0, 2).reshape(-1, n_chip * depth)
    return lax.dot_general(
        dest_token, returned, (((0,), (0,)), ((), ())), preferred_element_type=jnp.float32
    ).astype(jnp.bfloat16)


def one_window(pair, case, routes, gates, tokens, cotangent, weights, first_moment, second_moment):
    low, high = pair
    own_index = lax.axis_index("expert")
    active = (own_index == low) | (own_index == high)
    move = lambda block: lax.ppermute(block, "expert", [(low, high), (high, low)])
    bf16 = jnp.bfloat16
    first, second = first_moment[0], second_moment[0]
    depth = 2 * first.shape[0]

    block = jnp.where(active, move(weights[0]), weights[0])
    chip_weights = lax.all_gather(block, "core", axis=0, tiled=True)
    sends, pick = pick_rows(routes, gates, tokens, cotangent)
    got = exchange(sends.reshape(-1, 2 * CAP, depth), ACROSS)
    moments = jnp.concatenate((first, second)).astype(bf16)
    chip_weights, moments = lax.optimization_barrier((chip_weights, moments))
    rows_in = got[:, :CAP].reshape(-1, depth)
    grads_in = got[:, CAP:].reshape(-1, depth)
    mid = move(moments)
    shapes = jax.eval_shape(forward_backward, chip_weights, rows_in, grads_in)
    acts, part_rows = lax.cond(
        case >= 0,
        forward_backward,
        lambda *_: tuple(jnp.zeros(shape.shape, shape.dtype) for shape in shapes),
        chip_weights,
        rows_in,
        grads_in,
    )
    returned = send_back(part_rows)
    grad, other = weight_grads(rows_in, grads_in, acts, first.shape[0])
    new_first, new_second = update(
        active, lax.axis_index("core"), first, second, mid, grad, other
    )
    returned = returned.reshape(-1, depth)
    return combine(pick, returned, new_first), new_first[None], new_second[None]


def many_windows(tokens, cotangent, routes, gates, layout, weights, first_moment, second_moment):
    n_expert, n_chip = lax.axis_size("expert"), lax.axis_size(CHIPS)
    n_window = n_expert // HSPLIT
    own_index = lax.axis_index("expert")
    lane_ids = jnp.arange(n_expert, dtype=jnp.int32)
    placement, xor_mask, swap_on = layout[0], layout[1, 0], layout[2]
    held_slot = jnp.where(swap_on == 1, jnp.bitwise_xor(lane_ids, xor_mask), lane_ids)
    inverse = jnp.sum(
        jnp.where(placement[None, :] == lane_ids[:, None], lane_ids[None, :], 0), axis=1
    )
    slot_owner = inverse // HSPLIT
    expert_at = jnp.sum(
        jnp.where(held_slot[:, None] == lane_ids[None, :], slot_owner[None, :], 0), axis=1
    )
    active = select_lane(swap_on, lane_ids, own_index) == 1
    bf16 = jnp.bfloat16
    block = jnp.where(active, xor_rounds(weights[0], xor_mask), weights[0])
    moments = jnp.stack((first_moment[0], second_moment[0]))
    moved = xor_rounds(moments.astype(bf16), xor_mask).astype(jnp.float32)
    moments = jnp.where(active, moved, moments)

    tok_dev, top_count = routes.shape
    own_depth = weights.shape[1]
    depth = 2 * own_depth
    flat_ids = routes.reshape(-1)
    window_ids = jnp.arange(n_window, dtype=jnp.int32)
    hit_table = (flat_ids[:, None] == window_ids[None, :]).astype(jnp.int32)
    earlier = jnp.cumsum(hit_table, axis=0) - hit_table
    position = jnp.sum(earlier * hit_table, axis=1)
    kept = (flat_ids < n_window) & (position < CAP)
    slot_key = jnp.where(kept, flat_ids * CAP + position, -1)
    slot_pick = (jnp.arange(n_window * CAP, dtype=jnp.int32)[:, None] == slot_key[None, :]).astype(
        jnp.float32
    )
    assign_pick = slot_pick.reshape(n_window * CAP, tok_dev, top_count)
    slot_token = jnp.sum(assign_pick, axis=2)
    slot_gate = jnp.sum(assign_pick * gates[None], axis=(1, 2))[:, None]
    rows = jnp.dot(slot_token.astype(bf16), tokens, preferred_element_type=jnp.float32).astype(bf16)
    grads = jnp.dot(slot_token.astype(bf16), cotangent, preferred_element_type=jnp.float32)
    grads = (grads * slot_gate).astype(bf16)
    sends = jnp.stack((rows, grads)).reshape(2, n_window, CAP, n_chip, depth)
    sends = jnp.take(sends.transpose(3, 1, 0, 2, 4), expert_at, axis=1)
    dest_token = jnp.take(slot_token.reshape(n_window, CAP, tok_dev), expert_at, axis=0)
    dest_token = dest_token.reshape(n_expert * CAP, tok_dev).astype(bf16)
    got = exchange(sends.reshape(-1, 2 * CAP, depth), ACROSS)
    rows_in = got[:, :CAP].reshape(-1, depth)
    grads_in = got[:, CAP:].reshape(-1, depth)

    chip_weights = lax.all_gather(block, "core", axis=0, tiled=True)
    acts, part_rows = forward_backward(chip_weights, rows_in, grads_in)
    grad_input = add_up(send_back(part_rows), dest_token)
    grad, other = weight_grads(rows_in, grads_in, acts, own_depth)
    core = lax.axis_index("core")
    grad = jnp.where(core == 0, grad[:own_depth], grad[own_depth:]) + other.astype(jnp.float32)
    new_first = first_decay * moments[0] + (1.0 - first_decay) * grad
    new_second = second_decay * moments[1] + (1.0 - second_decay) * grad * grad
    return grad_input, new_first[None], new_second[None]


def local(tokens, cotangent, routes, gates, layout, weights, first_moment, second_moment):
    if lax.axis_size("expert") != HSPLIT:
        return many_windows(
            tokens, cotangent, routes, gates, layout, weights, first_moment, second_moment
        )
    case = swapping_pair(layout)
    branches = [functools.partial(one_window, pair) for pair in PAIRS]
    return lax.switch(
        case, branches, case, routes, gates, tokens, cotangent, weights, first_moment, second_moment
    )


def solution(mesh):
    n_dp, n_expert = mesh.devices.shape
    split = Mesh(mesh.devices.reshape(n_dp // 4, 2, 2, n_expert), ROWS)
    in_specs = (
        P(ROWS, None),
        P(ROWS, None),
        P(ROWS, None),
        P(ROWS, None),
        P(),
        P("expert", DP, None),
        P("expert", DP, None),
        P("expert", DP, None),
    )
    out_specs = (P(ROWS, None), P("expert", DP, None), P("expert", DP, None))
    return jax.shard_map(local, mesh=split, in_specs=in_specs, out_specs=out_specs, check_vma=False)
```

```python
import functools

import jax
import jax.numpy as jnp
from jax import lax
from jax.experimental import pallas as pl
from jax.experimental.pallas import tpu as pltpu
from jax.sharding import Mesh, PartitionSpec as P

HSPLIT = 4
CAP = 8


first_decay = 0.9
second_decay = 0.999

DP = ("outer", "inner", "core")
CHIPS = ("outer", "inner")
ROWS = DP + ("expert",)
ACROSS = CHIPS + ("expert",)
PAIRS = [(low, high) for low in range(4) for high in range(low + 1, 4)]


def xor_rounds(block, xor_mask):
    count = lax.axis_size("expert")
    for bit_pos in range(count.bit_length() - 1):
        route = [(lane, lane ^ (1 << bit_pos)) for lane in range(count)]
        partner_copy = lax.ppermute(block, "expert", route)
        flip_now = jnp.bitwise_and(jnp.right_shift(xor_mask, bit_pos), 1) == 1
        block = jnp.where(flip_now, partner_copy, block)
    return block


def select_lane(values, lane_ids, index_now):
    return jnp.sum(jnp.where(lane_ids == index_now, values, 0))


def exchange(block, axes):
    return lax.all_to_all(block, axes, split_axis=0, concat_axis=0, tiled=True)


def case_kernel(layout_ref, case_ref):
    case_ref[0, 0] = layout_ref[2, 1] - layout_ref[2, 0] + 2 * layout_ref[2, 2] + 3 * layout_ref[2, 3]


def swapping_pair(layout):
    smem = pl.BlockSpec(memory_space=pltpu.SMEM)
    return pl.pallas_call(
        case_kernel,
        out_shape=jax.ShapeDtypeStruct((1, 1), jnp.int32),
        in_specs=[smem],
        out_specs=smem,
        name="swapping_pair",
    )(layout)[0, 0]


def pick_kernel(routes_ref, gates_ref, tokens_ref, cot_ref, sends_ref, pick_ref):
    n_chip, n_expert, _, depth = sends_ref.shape
    tok_dev = tokens_ref.shape[0]
    hit = jnp.where(routes_ref[...] == 0, 1.0, 0.0)
    gate = jnp.sum(hit * gates_ref[...], axis=0, keepdims=True)
    hit = jnp.broadcast_to(jnp.sum(hit, axis=0, keepdims=True), (CAP, tok_dev))
    row_ids = lax.broadcasted_iota(jnp.int32, (tok_dev, tok_dev), 0)
    col_ids = lax.broadcasted_iota(jnp.int32, (tok_dev, tok_dev), 1)
    before = jnp.where(row_ids < col_ids, 1.0, 0.0).astype(jnp.bfloat16)
    position = jnp.dot(hit.astype(jnp.bfloat16), before, preferred_element_type=jnp.float32)
    slots = lax.broadcasted_iota(jnp.int32, (CAP, tok_dev), 0).astype(jnp.float32)
    pick = jnp.where(position == slots, hit, 0.0)
    slot_gate = jnp.sum(pick * gate, axis=1, keepdims=True)
    pick_ref[...] = jnp.concatenate((pick,) * n_expert, axis=0).T.astype(jnp.bfloat16)
    pick = pick.astype(jnp.bfloat16)
    for chip in range(n_chip):
        span = slice(chip * depth, (chip + 1) * depth)
        rows = jnp.dot(pick, tokens_ref[:, span], preferred_element_type=jnp.float32)
        grads = jnp.dot(pick, cot_ref[:, span], preferred_element_type=jnp.float32) * slot_gate
        both = jnp.concatenate((rows, grads), axis=0).astype(jnp.bfloat16)
        for expert in range(n_expert):
            sends_ref[chip, expert] = both


def pick_rows(routes, gates, tokens, cotangent):
    tok_dev, width = tokens.shape
    n_chip, n_expert = lax.axis_size(CHIPS), lax.axis_size("expert")
    vmem = pl.BlockSpec(memory_space=pltpu.VMEM)
    return pl.pallas_call(
        pick_kernel,
        out_shape=(
            jax.ShapeDtypeStruct((n_chip, n_expert, 2 * CAP, width // n_chip), jnp.bfloat16),
            jax.ShapeDtypeStruct((tok_dev, n_expert * CAP), jnp.bfloat16),
        ),
        in_specs=[vmem] * 4,
        out_specs=(vmem, vmem),
        cost_estimate=pl.CostEstimate(
            flops=4 * CAP * tok_dev * width, bytes_accessed=8 * tok_dev * width, transcendentals=0
        ),
        name="pick_rows",
    )(routes.T, gates.T, tokens, cotangent)


def grads_kernel(core_ref, got_ref, got_too_ref, acts_ref, acts_too_ref, out_ref):
    half, width = out_ref.shape
    wide = 2 * (width // 3)
    n_source, _, depth = got_ref.shape
    across = (((0,), (0,)), ((), ()))

    def run(base):
        span = slice(base, base + half)
        parts = [ref[:, :, span].astype(jnp.float32) for ref in (got_ref, got_too_ref)]
        got = jnp.concatenate(parts, axis=0)
        rows = got[:, :CAP].reshape(2 * n_source * CAP, half).astype(jnp.bfloat16)
        grads = got[:, CAP:].reshape(2 * n_source * CAP, half).astype(jnp.bfloat16)
        acts = jnp.concatenate((acts_ref[...], acts_too_ref[...]), axis=0)
        out_ref[:, :wide] = lax.dot_general(
            rows, acts[:, :wide], across, preferred_element_type=jnp.float32
        )
        out_ref[:, wide:] = lax.dot_general(
            grads, acts[:, wide:], across, preferred_element_type=jnp.float32
        )

    @pl.when(core_ref[0] == 0)
    def _():
        run(0)

    @pl.when(core_ref[0] == 1)
    def _():
        run(half)


def own_grads(got, got_too, acts, acts_too):
    vmem = pl.BlockSpec(memory_space=pltpu.VMEM)
    smem = pl.BlockSpec(memory_space=pltpu.SMEM)
    half, width = got.shape[2] // 2, acts.shape[1]
    return pl.pallas_call(
        grads_kernel,
        out_shape=jax.ShapeDtypeStruct((half, width), jnp.float32),
        in_specs=[smem] + [vmem] * 4,
        out_specs=vmem,
        cost_estimate=pl.CostEstimate(flops=5 * 10**9, bytes_accessed=8 * half * width, transcendentals=0),
        compiler_params=pltpu.CompilerParams(vmem_limit_bytes=12 << 20),
        name="own_grads",
    )(lax.axis_index("core").reshape(1), got, got_too, acts, acts_too)


def sibling(block):
    return lax.ppermute(block, "core", [(0, 1), (1, 0)])


def update_kernel(active_ref, first_ref, second_ref, moved_ref, grad_ref, new_first_ref, new_second_ref):
    rows = first_ref.shape[0]
    step = 16

    def write(pick_first, pick_second):
        for low in range(0, rows, step):
            span = slice(low, low + step)
            grad = grad_ref[span]
            new_first_ref[span] = first_decay * pick_first(span) + (1.0 - first_decay) * grad
            new_second_ref[span] = second_decay * pick_second(span) + (1.0 - second_decay) * grad * grad

    @pl.when(active_ref[0] == 1)
    def _():
        write(
            lambda span: moved_ref[span].astype(jnp.float32),
            lambda span: moved_ref[rows + span.start : rows + span.stop].astype(jnp.float32),
        )

    @pl.when(active_ref[0] == 0)
    def _():
        write(lambda span: first_ref[span], lambda span: second_ref[span])


def update(active, first, second, moved, grad):
    vmem = pl.BlockSpec(memory_space=pltpu.VMEM)
    smem = pl.BlockSpec(memory_space=pltpu.SMEM)
    return pl.pallas_call(
        update_kernel,
        out_shape=(jax.ShapeDtypeStruct(first.shape, jnp.float32),) * 2,
        in_specs=[smem] + [vmem] * 4,
        out_specs=(vmem, vmem),
        cost_estimate=pl.CostEstimate(
            flops=8 * first.size, bytes_accessed=24 * first.size, transcendentals=0
        ),
        compiler_params=pltpu.CompilerParams(vmem_limit_bytes=12 << 20),
        name="update",
    )(active.astype(jnp.int32).reshape(1), first, second, moved, grad)


def combine_kernel(pick_ref, returned_ref, first_ref, out_ref):
    slots = pick_ref.shape[1]
    depth = returned_ref.shape[1]
    for chip in range(returned_ref.shape[0] // slots):
        rows = returned_ref[chip * slots : (chip + 1) * slots]
        out_ref[:, chip * depth : (chip + 1) * depth] = jnp.dot(
            pick_ref[...], rows, preferred_element_type=jnp.float32
        ).astype(jnp.bfloat16)


def combine(pick, returned, first):
    tok_dev, slots = pick.shape
    rows, depth = returned.shape
    width = rows // slots * depth
    vmem, hbm = pl.BlockSpec(memory_space=pltpu.VMEM), pl.BlockSpec(memory_space=pl.ANY)
    return pl.pallas_call(
        combine_kernel,
        out_shape=jax.ShapeDtypeStruct((tok_dev, width), jnp.bfloat16),
        in_specs=[vmem, vmem, hbm],
        out_specs=vmem,
        cost_estimate=pl.CostEstimate(
            flops=2 * returned.size * tok_dev, bytes_accessed=4 * tok_dev * width, transcendentals=0
        ),
        compiler_params=pltpu.CompilerParams(vmem_limit_bytes=4 << 20),
        name="combine",
    )(pick, returned, first)


def forward_backward(chip_weights, rows_in, grads_in):
    n_chip = lax.axis_size(CHIPS)
    width_dev = chip_weights.shape[1] // 3
    bf16 = jnp.bfloat16
    pre_part = jnp.dot(rows_in, chip_weights[:, : 2 * width_dev], preferred_element_type=jnp.float32)
    grad_part = jnp.dot(grads_in, chip_weights[:, 2 * width_dev :], preferred_element_type=jnp.float32)
    parts = jnp.concatenate((pre_part, grad_part), axis=1).astype(bf16)
    if n_chip > 4:
        sums = exchange(parts.reshape(n_chip, -1, parts.shape[1]), CHIPS)
        sums = jnp.sum(sums.astype(jnp.float32), axis=0).astype(bf16)
        sums = lax.all_gather(sums, CHIPS, axis=0, tiled=True).astype(jnp.float32)
    else:
        sums = jnp.sum(lax.all_gather(parts, CHIPS, axis=0).astype(jnp.float32), axis=0)
    gate_pre = sums[:, :width_dev]
    up_pre = sums[:, width_dev : 2 * width_dev]
    hidden_grad = sums[:, 2 * width_dev :]
    sigma = jax.nn.sigmoid(gate_pre)
    active_part = gate_pre * sigma
    hidden = active_part * up_pre
    gate_grad = hidden_grad * up_pre * sigma * (1.0 + gate_pre * (1.0 - sigma))
    up_grad = hidden_grad * active_part
    acts = jnp.concatenate((gate_grad, up_grad, hidden), axis=1).astype(bf16)
    part_rows = lax.dot_general(
        acts[:, : 2 * width_dev],
        chip_weights[:, : 2 * width_dev],
        (((1,), (1,)), ((), ())),
        preferred_element_type=jnp.float32,
    ).astype(bf16)
    return acts, part_rows


def weight_grads(rows_in, grads_in, acts, own_depth):
    width_dev = acts.shape[1] // 3
    across = (((0,), (0,)), ((), ()))
    proj_grad = lax.dot_general(
        rows_in, acts[:, : 2 * width_dev], across, preferred_element_type=jnp.float32
    )
    down_grad = lax.dot_general(
        grads_in, acts[:, 2 * width_dev :], across, preferred_element_type=jnp.float32
    )
    grad = jnp.concatenate((proj_grad, down_grad), axis=1)
    low, high = grad[:own_depth], grad[own_depth:]
    core = lax.axis_index("core")
    other = lax.ppermute(
        jnp.where(core == 0, high, low).astype(jnp.bfloat16), "core", [(0, 1), (1, 0)]
    )
    return grad, other


def send_back(part_rows):
    return exchange(part_rows.reshape(lax.axis_size(ACROSS), CAP, part_rows.shape[1]), ACROSS)


def add_up(returned, dest_token):
    n_chip, depth = lax.axis_size(CHIPS), returned.shape[-1]
    returned = returned.reshape(n_chip, -1, depth).transpose(1, 0, 2).reshape(-1, n_chip * depth)
    return lax.dot_general(
        dest_token, returned, (((0,), (0,)), ((), ())), preferred_element_type=jnp.float32
    ).astype(jnp.bfloat16)


def always(case, part, *operands):
    shapes = jax.eval_shape(part, *operands)
    nothing = lambda *_: tuple(jnp.zeros(shape.shape, shape.dtype) for shape in shapes)
    return lax.cond(case >= 0, part, nothing, *operands)


def one_window(pair, case, routes, gates, tokens, cotangent, weights, first_moment, second_moment):
    low, high = pair
    own_index = lax.axis_index("expert")
    active = (own_index == low) | (own_index == high)
    move = lambda block: lax.ppermute(block, "expert", [(low, high), (high, low)])
    bf16 = jnp.bfloat16
    first, second = first_moment[0], second_moment[0]
    depth = 2 * first.shape[0]

    block = jnp.where(active, move(weights[0]), weights[0])
    chip_weights = lax.all_gather(block, "core", axis=0, tiled=True)
    sends, pick = pick_rows(routes, gates, tokens, cotangent)
    got = exchange(sends.reshape(-1, 2 * CAP, depth), ACROSS)
    moments = jnp.concatenate((first, second)).astype(bf16)
    chip_weights, moments = lax.optimization_barrier((chip_weights, moments))
    rows_in = got[:, :CAP].reshape(-1, depth)
    grads_in = got[:, CAP:].reshape(-1, depth)
    mid = move(moments)
    acts, part_rows = always(case, forward_backward, chip_weights, rows_in, grads_in)
    returned = send_back(part_rows)
    acts, got = lax.optimization_barrier((acts, got))
    grad = own_grads(got, sibling(got), acts, sibling(acts))
    new_first, new_second = update(active, first, second, mid, grad)
    returned = returned.reshape(-1, depth)
    return combine(pick, returned, new_first), new_first[None], new_second[None]


def many_windows(tokens, cotangent, routes, gates, layout, weights, first_moment, second_moment):
    n_expert, n_chip = lax.axis_size("expert"), lax.axis_size(CHIPS)
    n_window = n_expert // HSPLIT
    own_index = lax.axis_index("expert")
    lane_ids = jnp.arange(n_expert, dtype=jnp.int32)
    placement, xor_mask, swap_on = layout[0], layout[1, 0], layout[2]
    held_slot = jnp.where(swap_on == 1, jnp.bitwise_xor(lane_ids, xor_mask), lane_ids)
    inverse = jnp.sum(
        jnp.where(placement[None, :] == lane_ids[:, None], lane_ids[None, :], 0), axis=1
    )
    slot_owner = inverse // HSPLIT
    expert_at = jnp.sum(
        jnp.where(held_slot[:, None] == lane_ids[None, :], slot_owner[None, :], 0), axis=1
    )
    active = select_lane(swap_on, lane_ids, own_index) == 1
    bf16 = jnp.bfloat16
    block = jnp.where(active, xor_rounds(weights[0], xor_mask), weights[0])
    moments = jnp.stack((first_moment[0], second_moment[0]))
    moved = xor_rounds(moments.astype(bf16), xor_mask).astype(jnp.float32)
    moments = jnp.where(active, moved, moments)

    tok_dev, top_count = routes.shape
    own_depth = weights.shape[1]
    depth = 2 * own_depth
    flat_ids = routes.reshape(-1)
    window_ids = jnp.arange(n_window, dtype=jnp.int32)
    hit_table = (flat_ids[:, None] == window_ids[None, :]).astype(jnp.int32)
    earlier = jnp.cumsum(hit_table, axis=0) - hit_table
    position = jnp.sum(earlier * hit_table, axis=1)
    kept = (flat_ids < n_window) & (position < CAP)
    slot_key = jnp.where(kept, flat_ids * CAP + position, -1)
    slot_pick = (jnp.arange(n_window * CAP, dtype=jnp.int32)[:, None] == slot_key[None, :]).astype(
        jnp.float32
    )
    assign_pick = slot_pick.reshape(n_window * CAP, tok_dev, top_count)
    slot_token = jnp.sum(assign_pick, axis=2)
    slot_gate = jnp.sum(assign_pick * gates[None], axis=(1, 2))[:, None]
    rows = jnp.dot(slot_token.astype(bf16), tokens, preferred_element_type=jnp.float32).astype(bf16)
    grads = jnp.dot(slot_token.astype(bf16), cotangent, preferred_element_type=jnp.float32)
    grads = (grads * slot_gate).astype(bf16)
    sends = jnp.stack((rows, grads)).reshape(2, n_window, CAP, n_chip, depth)
    sends = jnp.take(sends.transpose(3, 1, 0, 2, 4), expert_at, axis=1)
    dest_token = jnp.take(slot_token.reshape(n_window, CAP, tok_dev), expert_at, axis=0)
    dest_token = dest_token.reshape(n_expert * CAP, tok_dev).astype(bf16)
    got = exchange(sends.reshape(-1, 2 * CAP, depth), ACROSS)
    rows_in = got[:, :CAP].reshape(-1, depth)
    grads_in = got[:, CAP:].reshape(-1, depth)

    chip_weights = lax.all_gather(block, "core", axis=0, tiled=True)
    acts, part_rows = forward_backward(chip_weights, rows_in, grads_in)
    grad_input = add_up(send_back(part_rows), dest_token)
    grad, other = weight_grads(rows_in, grads_in, acts, own_depth)
    core = lax.axis_index("core")
    grad = jnp.where(core == 0, grad[:own_depth], grad[own_depth:]) + other.astype(jnp.float32)
    new_first = first_decay * moments[0] + (1.0 - first_decay) * grad
    new_second = second_decay * moments[1] + (1.0 - second_decay) * grad * grad
    return grad_input, new_first[None], new_second[None]


def local(tokens, cotangent, routes, gates, layout, weights, first_moment, second_moment):
    if lax.axis_size("expert") != HSPLIT:
        return many_windows(
            tokens, cotangent, routes, gates, layout, weights, first_moment, second_moment
        )
    case = swapping_pair(layout)
    branches = [functools.partial(one_window, pair) for pair in PAIRS]
    return lax.switch(
        case, branches, case, routes, gates, tokens, cotangent, weights, first_moment, second_moment
    )


def solution(mesh):
    n_dp, n_expert = mesh.devices.shape
    split = Mesh(mesh.devices.reshape(n_dp // 4, 2, 2, n_expert), ROWS)
    in_specs = (
        P(ROWS, None),
        P(ROWS, None),
        P(ROWS, None),
        P(ROWS, None),
        P(),
        P("expert", DP, None),
        P("expert", DP, None),
        P("expert", DP, None),
    )
    out_specs = (P(ROWS, None), P("expert", DP, None), P("expert", DP, None))
    return jax.shard_map(local, mesh=split, in_specs=in_specs, out_specs=out_specs, check_vma=False)
```

```python
import functools

import jax
import jax.numpy as jnp
from jax import lax
from jax.experimental import pallas as pl
from jax.experimental.pallas import tpu as pltpu
from jax.sharding import Mesh, PartitionSpec as P

HSPLIT = 4
CAP = 8


first_decay = 0.9
second_decay = 0.999

DP = ("outer", "inner", "core")
CHIPS = ("outer", "inner")
ROWS = DP + ("expert",)
ACROSS = CHIPS + ("expert",)
MIXED = ("outer", "expert", "inner")
PAIRS = [(low, high) for low in range(4) for high in range(low + 1, 4)]


def xor_rounds(block, xor_mask):
    count = lax.axis_size("expert")
    for bit_pos in range(count.bit_length() - 1):
        route = [(lane, lane ^ (1 << bit_pos)) for lane in range(count)]
        partner_copy = lax.ppermute(block, "expert", route)
        flip_now = jnp.bitwise_and(jnp.right_shift(xor_mask, bit_pos), 1) == 1
        block = jnp.where(flip_now, partner_copy, block)
    return block


def select_lane(values, lane_ids, index_now):
    return jnp.sum(jnp.where(lane_ids == index_now, values, 0))


def exchange(block, axes):
    return lax.all_to_all(block, axes, split_axis=0, concat_axis=0, tiled=True)


def case_kernel(layout_ref, case_ref):
    case_ref[0, 0] = layout_ref[2, 1] - layout_ref[2, 0] + 2 * layout_ref[2, 2] + 3 * layout_ref[2, 3]


def swapping_pair(layout):
    smem = pl.BlockSpec(memory_space=pltpu.SMEM)
    return pl.pallas_call(
        case_kernel,
        out_shape=jax.ShapeDtypeStruct((1, 1), jnp.int32),
        in_specs=[smem],
        out_specs=smem,
        name="swapping_pair",
    )(layout)[0, 0]


def pick_kernel(routes_ref, gates_ref, tokens_ref, cot_ref, sends_ref, pick_ref):
    n_outer, n_expert, n_inner, _, depth = sends_ref.shape
    n_chip = n_outer * n_inner
    tok_dev = tokens_ref.shape[0]
    hit = jnp.where(routes_ref[...] == 0, 1.0, 0.0)
    gate = jnp.sum(hit * gates_ref[...], axis=0, keepdims=True)
    hit = jnp.broadcast_to(jnp.sum(hit, axis=0, keepdims=True), (CAP, tok_dev))
    row_ids = lax.broadcasted_iota(jnp.int32, (tok_dev, tok_dev), 0)
    col_ids = lax.broadcasted_iota(jnp.int32, (tok_dev, tok_dev), 1)
    before = jnp.where(row_ids < col_ids, 1.0, 0.0).astype(jnp.bfloat16)
    position = jnp.dot(hit.astype(jnp.bfloat16), before, preferred_element_type=jnp.float32)
    slots = lax.broadcasted_iota(jnp.int32, (CAP, tok_dev), 0).astype(jnp.float32)
    pick = jnp.where(position == slots, hit, 0.0)
    slot_gate = jnp.sum(pick * gate, axis=1, keepdims=True)
    none = jnp.zeros_like(pick)
    for inner in range(n_inner):
        blocks = [pick if other == inner else none for other in range(n_inner)] * n_expert
        pick_ref[inner] = jnp.concatenate(blocks, axis=0).T.astype(jnp.bfloat16)
    pick = pick.astype(jnp.bfloat16)
    for chip in range(n_chip):
        span = slice(chip * depth, (chip + 1) * depth)
        rows = jnp.dot(pick, tokens_ref[:, span], preferred_element_type=jnp.float32)
        grads = jnp.dot(pick, cot_ref[:, span], preferred_element_type=jnp.float32) * slot_gate
        both = jnp.concatenate((rows, grads), axis=0).astype(jnp.bfloat16)
        for expert in range(n_expert):
            sends_ref[chip // n_inner, expert, chip % n_inner] = both


def pick_rows(routes, gates, tokens, cotangent):
    tok_dev, width = tokens.shape
    n_outer, n_inner = lax.axis_size("outer"), lax.axis_size("inner")
    n_chip, n_expert = n_outer * n_inner, lax.axis_size("expert")
    vmem = pl.BlockSpec(memory_space=pltpu.VMEM)
    return pl.pallas_call(
        pick_kernel,
        out_shape=(
            jax.ShapeDtypeStruct((n_outer, n_expert, n_inner, 2 * CAP, width // n_chip), jnp.bfloat16),
            jax.ShapeDtypeStruct((n_inner, tok_dev, n_expert * n_inner * CAP), jnp.bfloat16),
        ),
        in_specs=[vmem] * 4,
        out_specs=(vmem, vmem),
        cost_estimate=pl.CostEstimate(
            flops=4 * CAP * tok_dev * width, bytes_accessed=8 * tok_dev * width, transcendentals=0
        ),
        name="pick_rows",
    )(routes.T, gates.T, tokens, cotangent)


def grads_kernel(core_ref, got_ref, got_too_ref, acts_ref, acts_too_ref, out_ref):
    half, width = out_ref.shape
    wide = 2 * (width // 3)
    n_source, _, depth = got_ref.shape
    across = (((0,), (0,)), ((), ()))

    def run(base):
        span = slice(base, base + half)
        parts = [ref[:, :, span].astype(jnp.float32) for ref in (got_ref, got_too_ref)]
        got = jnp.concatenate(parts, axis=0)
        rows = got[:, :CAP].reshape(2 * n_source * CAP, half).astype(jnp.bfloat16)
        grads = got[:, CAP:].reshape(2 * n_source * CAP, half).astype(jnp.bfloat16)
        acts = jnp.concatenate((acts_ref[...], acts_too_ref[...]), axis=0)
        out_ref[:, :wide] = lax.dot_general(
            rows, acts[:, :wide], across, preferred_element_type=jnp.float32
        )
        out_ref[:, wide:] = lax.dot_general(
            grads, acts[:, wide:], across, preferred_element_type=jnp.float32
        )

    @pl.when(core_ref[0] == 0)
    def _():
        run(0)

    @pl.when(core_ref[0] == 1)
    def _():
        run(half)


def own_grads(got, got_too, acts, acts_too):
    vmem = pl.BlockSpec(memory_space=pltpu.VMEM)
    smem = pl.BlockSpec(memory_space=pltpu.SMEM)
    half, width = got.shape[2] // 2, acts.shape[1]
    return pl.pallas_call(
        grads_kernel,
        out_shape=jax.ShapeDtypeStruct((half, width), jnp.float32),
        in_specs=[smem] + [vmem] * 4,
        out_specs=vmem,
        cost_estimate=pl.CostEstimate(flops=5 * 10**9, bytes_accessed=8 * half * width, transcendentals=0),
        compiler_params=pltpu.CompilerParams(vmem_limit_bytes=12 << 20),
        name="own_grads",
    )(lax.axis_index("core").reshape(1), got, got_too, acts, acts_too)


def sibling(block):
    return lax.ppermute(block, "core", [(0, 1), (1, 0)])


def update_kernel(active_ref, first_ref, second_ref, moved_ref, grad_ref, new_first_ref, new_second_ref):
    rows = first_ref.shape[0]
    step = 16

    def write(pick_first, pick_second):
        for low in range(0, rows, step):
            span = slice(low, low + step)
            grad = grad_ref[span]
            new_first_ref[span] = first_decay * pick_first(span) + (1.0 - first_decay) * grad
            new_second_ref[span] = second_decay * pick_second(span) + (1.0 - second_decay) * grad * grad

    @pl.when(active_ref[0] == 1)
    def _():
        write(
            lambda span: moved_ref[span].astype(jnp.float32),
            lambda span: moved_ref[rows + span.start : rows + span.stop].astype(jnp.float32),
        )

    @pl.when(active_ref[0] == 0)
    def _():
        write(lambda span: first_ref[span], lambda span: second_ref[span])


def update(active, first, second, moved, grad):
    vmem = pl.BlockSpec(memory_space=pltpu.VMEM)
    smem = pl.BlockSpec(memory_space=pltpu.SMEM)
    return pl.pallas_call(
        update_kernel,
        out_shape=(jax.ShapeDtypeStruct(first.shape, jnp.float32),) * 2,
        in_specs=[smem] + [vmem] * 4,
        out_specs=(vmem, vmem),
        cost_estimate=pl.CostEstimate(
            flops=8 * first.size, bytes_accessed=24 * first.size, transcendentals=0
        ),
        compiler_params=pltpu.CompilerParams(vmem_limit_bytes=12 << 20),
        name="update",
    )(active.astype(jnp.int32).reshape(1), first, second, moved, grad)


def combine_kernel(pick_ref, returned_ref, first_ref, out_ref):
    n_inner, _, slots = pick_ref.shape
    depth = returned_ref.shape[1]
    for chip in range(returned_ref.shape[0] // slots * n_inner):
        outer, inner = chip // n_inner, chip % n_inner
        rows = returned_ref[outer * slots : (outer + 1) * slots]
        out_ref[:, chip * depth : (chip + 1) * depth] = jnp.dot(
            pick_ref[inner], rows, preferred_element_type=jnp.float32
        ).astype(jnp.bfloat16)


def combine(pick, returned, first):
    n_inner, tok_dev, slots = pick.shape
    rows, depth = returned.shape
    width = rows // slots * n_inner * depth
    vmem, hbm = pl.BlockSpec(memory_space=pltpu.VMEM), pl.BlockSpec(memory_space=pl.ANY)
    return pl.pallas_call(
        combine_kernel,
        out_shape=jax.ShapeDtypeStruct((tok_dev, width), jnp.bfloat16),
        in_specs=[vmem, vmem, hbm],
        out_specs=vmem,
        cost_estimate=pl.CostEstimate(
            flops=2 * returned.size * tok_dev, bytes_accessed=4 * tok_dev * width, transcendentals=0
        ),
        compiler_params=pltpu.CompilerParams(vmem_limit_bytes=4 << 20),
        name="combine",
    )(pick, returned, first)


def forward_backward(chip_weights, rows_in, grads_in):
    n_chip = lax.axis_size(CHIPS)
    width_dev = chip_weights.shape[1] // 3
    bf16 = jnp.bfloat16
    pre_part = jnp.dot(rows_in, chip_weights[:, : 2 * width_dev], preferred_element_type=jnp.float32)
    grad_part = jnp.dot(grads_in, chip_weights[:, 2 * width_dev :], preferred_element_type=jnp.float32)
    parts = jnp.concatenate((pre_part, grad_part), axis=1).astype(bf16)
    if n_chip > 4:
        sums = exchange(parts.reshape(n_chip, -1, parts.shape[1]), CHIPS)
        sums = jnp.sum(sums.astype(jnp.float32), axis=0).astype(bf16)
        sums = lax.all_gather(sums, CHIPS, axis=0, tiled=True).astype(jnp.float32)
    else:
        sums = jnp.sum(lax.all_gather(parts, CHIPS, axis=0).astype(jnp.float32), axis=0)
    gate_pre = sums[:, :width_dev]
    up_pre = sums[:, width_dev : 2 * width_dev]
    hidden_grad = sums[:, 2 * width_dev :]
    sigma = jax.nn.sigmoid(gate_pre)
    active_part = gate_pre * sigma
    hidden = active_part * up_pre
    gate_grad = hidden_grad * up_pre * sigma * (1.0 + gate_pre * (1.0 - sigma))
    up_grad = hidden_grad * active_part
    acts = jnp.concatenate((gate_grad, up_grad, hidden), axis=1).astype(bf16)
    part_rows = lax.dot_general(
        acts[:, : 2 * width_dev],
        chip_weights[:, : 2 * width_dev],
        (((1,), (1,)), ((), ())),
        preferred_element_type=jnp.float32,
    ).astype(bf16)
    return acts, part_rows


def weight_grads(rows_in, grads_in, acts, own_depth):
    width_dev = acts.shape[1] // 3
    across = (((0,), (0,)), ((), ()))
    proj_grad = lax.dot_general(
        rows_in, acts[:, : 2 * width_dev], across, preferred_element_type=jnp.float32
    )
    down_grad = lax.dot_general(
        grads_in, acts[:, 2 * width_dev :], across, preferred_element_type=jnp.float32
    )
    grad = jnp.concatenate((proj_grad, down_grad), axis=1)
    low, high = grad[:own_depth], grad[own_depth:]
    core = lax.axis_index("core")
    other = lax.ppermute(
        jnp.where(core == 0, high, low).astype(jnp.bfloat16), "core", [(0, 1), (1, 0)]
    )
    return grad, other


def send_back(part_rows, axes):
    return exchange(part_rows.reshape(lax.axis_size(axes), CAP, part_rows.shape[1]), axes)


def add_up(returned, dest_token):
    n_chip, depth = lax.axis_size(CHIPS), returned.shape[-1]
    returned = returned.reshape(n_chip, -1, depth).transpose(1, 0, 2).reshape(-1, n_chip * depth)
    return lax.dot_general(
        dest_token, returned, (((0,), (0,)), ((), ())), preferred_element_type=jnp.float32
    ).astype(jnp.bfloat16)


def always(case, part, *operands):
    shapes = jax.eval_shape(part, *operands)
    nothing = lambda *_: tuple(jnp.zeros(shape.shape, shape.dtype) for shape in shapes)
    return lax.cond(case >= 0, part, nothing, *operands)


def one_window(pair, case, routes, gates, tokens, cotangent, weights, first_moment, second_moment):
    low, high = pair
    own_index = lax.axis_index("expert")
    active = (own_index == low) | (own_index == high)
    move = lambda block: lax.ppermute(block, "expert", [(low, high), (high, low)])
    bf16 = jnp.bfloat16
    first, second = first_moment[0], second_moment[0]
    depth = 2 * first.shape[0]

    block = jnp.where(active, move(weights[0]), weights[0])
    chip_weights = lax.all_gather(block, "core", axis=0, tiled=True)
    sends, pick = pick_rows(routes, gates, tokens, cotangent)
    got = exchange(sends.reshape(-1, 2 * CAP, depth), MIXED)
    moments = jnp.concatenate((first, second)).astype(bf16)
    chip_weights, moments = lax.optimization_barrier((chip_weights, moments))
    rows_in = got[:, :CAP].reshape(-1, depth)
    grads_in = got[:, CAP:].reshape(-1, depth)
    mid = move(moments)
    acts, part_rows = always(case, forward_backward, chip_weights, rows_in, grads_in)
    returned = send_back(part_rows, MIXED)
    acts, got = lax.optimization_barrier((acts, got))
    grad = own_grads(got, sibling(got), acts, sibling(acts))
    new_first, new_second = update(active, first, second, mid, grad)
    returned = returned.reshape(-1, depth)
    return combine(pick, returned, new_first), new_first[None], new_second[None]


def many_windows(tokens, cotangent, routes, gates, layout, weights, first_moment, second_moment):
    n_expert, n_chip = lax.axis_size("expert"), lax.axis_size(CHIPS)
    n_window = n_expert // HSPLIT
    own_index = lax.axis_index("expert")
    lane_ids = jnp.arange(n_expert, dtype=jnp.int32)
    placement, xor_mask, swap_on = layout[0], layout[1, 0], layout[2]
    held_slot = jnp.where(swap_on == 1, jnp.bitwise_xor(lane_ids, xor_mask), lane_ids)
    inverse = jnp.sum(
        jnp.where(placement[None, :] == lane_ids[:, None], lane_ids[None, :], 0), axis=1
    )
    slot_owner = inverse // HSPLIT
    expert_at = jnp.sum(
        jnp.where(held_slot[:, None] == lane_ids[None, :], slot_owner[None, :], 0), axis=1
    )
    active = select_lane(swap_on, lane_ids, own_index) == 1
    bf16 = jnp.bfloat16
    block = jnp.where(active, xor_rounds(weights[0], xor_mask), weights[0])
    moments = jnp.stack((first_moment[0], second_moment[0]))
    moved = xor_rounds(moments.astype(bf16), xor_mask).astype(jnp.float32)
    moments = jnp.where(active, moved, moments)

    tok_dev, top_count = routes.shape
    own_depth = weights.shape[1]
    depth = 2 * own_depth
    flat_ids = routes.reshape(-1)
    window_ids = jnp.arange(n_window, dtype=jnp.int32)
    hit_table = (flat_ids[:, None] == window_ids[None, :]).astype(jnp.int32)
    earlier = jnp.cumsum(hit_table, axis=0) - hit_table
    position = jnp.sum(earlier * hit_table, axis=1)
    kept = (flat_ids < n_window) & (position < CAP)
    slot_key = jnp.where(kept, flat_ids * CAP + position, -1)
    slot_pick = (jnp.arange(n_window * CAP, dtype=jnp.int32)[:, None] == slot_key[None, :]).astype(
        jnp.float32
    )
    assign_pick = slot_pick.reshape(n_window * CAP, tok_dev, top_count)
    slot_token = jnp.sum(assign_pick, axis=2)
    slot_gate = jnp.sum(assign_pick * gates[None], axis=(1, 2))[:, None]
    rows = jnp.dot(slot_token.astype(bf16), tokens, preferred_element_type=jnp.float32).astype(bf16)
    grads = jnp.dot(slot_token.astype(bf16), cotangent, preferred_element_type=jnp.float32)
    grads = (grads * slot_gate).astype(bf16)
    sends = jnp.stack((rows, grads)).reshape(2, n_window, CAP, n_chip, depth)
    sends = jnp.take(sends.transpose(3, 1, 0, 2, 4), expert_at, axis=1)
    dest_token = jnp.take(slot_token.reshape(n_window, CAP, tok_dev), expert_at, axis=0)
    dest_token = dest_token.reshape(n_expert * CAP, tok_dev).astype(bf16)
    got = exchange(sends.reshape(-1, 2 * CAP, depth), ACROSS)
    rows_in = got[:, :CAP].reshape(-1, depth)
    grads_in = got[:, CAP:].reshape(-1, depth)

    chip_weights = lax.all_gather(block, "core", axis=0, tiled=True)
    acts, part_rows = forward_backward(chip_weights, rows_in, grads_in)
    grad_input = add_up(send_back(part_rows, ACROSS), dest_token)
    grad, other = weight_grads(rows_in, grads_in, acts, own_depth)
    core = lax.axis_index("core")
    grad = jnp.where(core == 0, grad[:own_depth], grad[own_depth:]) + other.astype(jnp.float32)
    new_first = first_decay * moments[0] + (1.0 - first_decay) * grad
    new_second = second_decay * moments[1] + (1.0 - second_decay) * grad * grad
    return grad_input, new_first[None], new_second[None]


def local(tokens, cotangent, routes, gates, layout, weights, first_moment, second_moment):
    if lax.axis_size("expert") != HSPLIT:
        return many_windows(
            tokens, cotangent, routes, gates, layout, weights, first_moment, second_moment
        )
    case = swapping_pair(layout)
    branches = [functools.partial(one_window, pair) for pair in PAIRS]
    return lax.switch(
        case, branches, case, routes, gates, tokens, cotangent, weights, first_moment, second_moment
    )


def solution(mesh):
    n_dp, n_expert = mesh.devices.shape
    split = Mesh(mesh.devices.reshape(n_dp // 4, 2, 2, n_expert), ROWS)
    in_specs = (
        P(ROWS, None),
        P(ROWS, None),
        P(ROWS, None),
        P(ROWS, None),
        P(),
        P("expert", DP, None),
        P("expert", DP, None),
        P("expert", DP, None),
    )
    out_specs = (P(ROWS, None), P("expert", DP, None), P("expert", DP, None))
    return jax.shard_map(local, mesh=split, in_specs=in_specs, out_specs=out_specs, check_vma=False)
```

```python
import functools

import jax
import jax.numpy as jnp
from jax import lax
from jax.experimental import pallas as pl
from jax.experimental.pallas import tpu as pltpu
from jax.sharding import Mesh, PartitionSpec as P

HSPLIT = 4
CAP = 8


first_decay = 0.9
second_decay = 0.999

DP = ("outer", "inner", "core")
CHIPS = ("outer", "inner")
ROWS = DP + ("expert",)
ACROSS = CHIPS + ("expert",)
MIXED = ("outer", "expert", "inner")
PAIRS = [(low, high) for low in range(4) for high in range(low + 1, 4)]


def xor_rounds(block, xor_mask):
    count = lax.axis_size("expert")
    for bit_pos in range(count.bit_length() - 1):
        route = [(lane, lane ^ (1 << bit_pos)) for lane in range(count)]
        partner_copy = lax.ppermute(block, "expert", route)
        flip_now = jnp.bitwise_and(jnp.right_shift(xor_mask, bit_pos), 1) == 1
        block = jnp.where(flip_now, partner_copy, block)
    return block


def select_lane(values, lane_ids, index_now):
    return jnp.sum(jnp.where(lane_ids == index_now, values, 0))


def exchange(block, axes):
    return lax.all_to_all(block, axes, split_axis=0, concat_axis=0, tiled=True)


def case_kernel(layout_ref, case_ref):
    case_ref[0, 0] = layout_ref[2, 1] - layout_ref[2, 0] + 2 * layout_ref[2, 2] + 3 * layout_ref[2, 3]


def swapping_pair(layout):
    smem = pl.BlockSpec(memory_space=pltpu.SMEM)
    return pl.pallas_call(
        case_kernel,
        out_shape=jax.ShapeDtypeStruct((1, 1), jnp.int32),
        in_specs=[smem],
        out_specs=smem,
        name="swapping_pair",
    )(layout)[0, 0]


def pick_kernel(routes_ref, gates_ref, tokens_ref, cot_ref, sends_ref, pick_ref):
    n_outer, n_expert, n_inner, _, depth = sends_ref.shape
    n_chip = n_outer * n_inner
    tok_dev = tokens_ref.shape[0]
    hit = jnp.where(routes_ref[...] == 0, 1.0, 0.0)
    gate = jnp.sum(hit * gates_ref[...], axis=0, keepdims=True)
    hit = jnp.broadcast_to(jnp.sum(hit, axis=0, keepdims=True), (CAP, tok_dev))
    row_ids = lax.broadcasted_iota(jnp.int32, (tok_dev, tok_dev), 0)
    col_ids = lax.broadcasted_iota(jnp.int32, (tok_dev, tok_dev), 1)
    before = jnp.where(row_ids < col_ids, 1.0, 0.0).astype(jnp.bfloat16)
    position = jnp.dot(hit.astype(jnp.bfloat16), before, preferred_element_type=jnp.float32)
    slots = lax.broadcasted_iota(jnp.int32, (CAP, tok_dev), 0).astype(jnp.float32)
    pick = jnp.where(position == slots, hit, 0.0)
    slot_gate = jnp.sum(pick * gate, axis=1, keepdims=True)
    none = jnp.zeros_like(pick)
    for inner in range(n_inner):
        blocks = [pick if other == inner else none for other in range(n_inner)] * n_expert
        pick_ref[inner] = jnp.concatenate(blocks, axis=0).T.astype(jnp.bfloat16)
    pick = pick.astype(jnp.bfloat16)
    for chip in range(n_chip):
        span = slice(chip * depth, (chip + 1) * depth)
        rows = jnp.dot(pick, tokens_ref[:, span], preferred_element_type=jnp.float32)
        grads = jnp.dot(pick, cot_ref[:, span], preferred_element_type=jnp.float32) * slot_gate
        both = jnp.concatenate((rows, grads), axis=0).astype(jnp.bfloat16)
        for expert in range(n_expert):
            sends_ref[chip // n_inner, expert, chip % n_inner] = both


def pick_rows(routes, gates, tokens, cotangent):
    tok_dev, width = tokens.shape
    n_outer, n_inner = lax.axis_size("outer"), lax.axis_size("inner")
    n_chip, n_expert = n_outer * n_inner, lax.axis_size("expert")
    vmem = pl.BlockSpec(memory_space=pltpu.VMEM)
    return pl.pallas_call(
        pick_kernel,
        out_shape=(
            jax.ShapeDtypeStruct((n_outer, n_expert, n_inner, 2 * CAP, width // n_chip), jnp.bfloat16),
            jax.ShapeDtypeStruct((n_inner, tok_dev, n_expert * n_inner * CAP), jnp.bfloat16),
        ),
        in_specs=[vmem] * 4,
        out_specs=(vmem, vmem),
        cost_estimate=pl.CostEstimate(
            flops=4 * CAP * tok_dev * width, bytes_accessed=8 * tok_dev * width, transcendentals=0
        ),
        name="pick_rows",
    )(routes.T, gates.T, tokens, cotangent)


def grads_kernel(core_ref, got_ref, got_too_ref, acts_ref, acts_too_ref, out_ref):
    half, width = out_ref.shape
    wide = 2 * (width // 3)
    n_source, _, depth = got_ref.shape
    across = (((0,), (0,)), ((), ()))

    def run(base):
        span = slice(base, base + half)
        parts = [ref[:, :, span].astype(jnp.float32) for ref in (got_ref, got_too_ref)]
        got = jnp.concatenate(parts, axis=0)
        rows = got[:, :CAP].reshape(2 * n_source * CAP, half).astype(jnp.bfloat16)
        grads = got[:, CAP:].reshape(2 * n_source * CAP, half).astype(jnp.bfloat16)
        acts = jnp.concatenate((acts_ref[...], acts_too_ref[...]), axis=0)
        out_ref[:, :wide] = lax.dot_general(
            rows, acts[:, :wide], across, preferred_element_type=jnp.float32
        )
        out_ref[:, wide:] = lax.dot_general(
            grads, acts[:, wide:], across, preferred_element_type=jnp.float32
        )

    @pl.when(core_ref[0] == 0)
    def _():
        run(0)

    @pl.when(core_ref[0] == 1)
    def _():
        run(half)


def own_grads(got, got_too, acts, acts_too):
    vmem = pl.BlockSpec(memory_space=pltpu.VMEM)
    smem = pl.BlockSpec(memory_space=pltpu.SMEM)
    half, width = got.shape[2] // 2, acts.shape[1]
    return pl.pallas_call(
        grads_kernel,
        out_shape=jax.ShapeDtypeStruct((half, width), jnp.float32),
        in_specs=[smem] + [vmem] * 4,
        out_specs=vmem,
        cost_estimate=pl.CostEstimate(flops=5 * 10**9, bytes_accessed=8 * half * width, transcendentals=0),
        compiler_params=pltpu.CompilerParams(vmem_limit_bytes=12 << 20),
        name="own_grads",
    )(lax.axis_index("core").reshape(1), got, got_too, acts, acts_too)


def sibling(block):
    return lax.ppermute(block, "core", [(0, 1), (1, 0)])


def update_kernel(active_ref, first_ref, second_ref, moved_ref, grad_ref, new_first_ref, new_second_ref):
    rows = first_ref.shape[0]
    step = 16

    def write(pick_first, pick_second):
        for low in range(0, rows, step):
            span = slice(low, low + step)
            grad = grad_ref[span]
            new_first_ref[span] = first_decay * pick_first(span) + (1.0 - first_decay) * grad
            new_second_ref[span] = second_decay * pick_second(span) + (1.0 - second_decay) * grad * grad

    @pl.when(active_ref[0] == 1)
    def _():
        write(
            lambda span: moved_ref[span].astype(jnp.float32),
            lambda span: moved_ref[rows + span.start : rows + span.stop].astype(jnp.float32),
        )

    @pl.when(active_ref[0] == 0)
    def _():
        write(lambda span: first_ref[span], lambda span: second_ref[span])


def update(active, first, second, moved, grad):
    vmem = pl.BlockSpec(memory_space=pltpu.VMEM)
    smem = pl.BlockSpec(memory_space=pltpu.SMEM)
    return pl.pallas_call(
        update_kernel,
        out_shape=(jax.ShapeDtypeStruct(first.shape, jnp.float32),) * 2,
        in_specs=[smem] + [vmem] * 4,
        out_specs=(vmem, vmem),
        cost_estimate=pl.CostEstimate(
            flops=8 * first.size, bytes_accessed=24 * first.size, transcendentals=0
        ),
        compiler_params=pltpu.CompilerParams(vmem_limit_bytes=12 << 20),
        name="update",
    )(active.astype(jnp.int32).reshape(1), first, second, moved, grad)


def combine_kernel(pick_ref, returned_ref, first_ref, out_ref):
    n_inner, _, slots = pick_ref.shape
    depth = returned_ref.shape[1]
    for chip in range(returned_ref.shape[0] // slots * n_inner):
        outer, inner = chip // n_inner, chip % n_inner
        rows = returned_ref[outer * slots : (outer + 1) * slots]
        out_ref[:, chip * depth : (chip + 1) * depth] = jnp.dot(
            pick_ref[inner], rows, preferred_element_type=jnp.float32
        ).astype(jnp.bfloat16)


def combine(pick, returned, first):
    n_inner, tok_dev, slots = pick.shape
    rows, depth = returned.shape
    width = rows // slots * n_inner * depth
    vmem, hbm = pl.BlockSpec(memory_space=pltpu.VMEM), pl.BlockSpec(memory_space=pl.ANY)
    return pl.pallas_call(
        combine_kernel,
        out_shape=jax.ShapeDtypeStruct((tok_dev, width), jnp.bfloat16),
        in_specs=[vmem, vmem, hbm],
        out_specs=vmem,
        cost_estimate=pl.CostEstimate(
            flops=2 * returned.size * tok_dev, bytes_accessed=4 * tok_dev * width, transcendentals=0
        ),
        compiler_params=pltpu.CompilerParams(vmem_limit_bytes=4 << 20),
        name="combine",
    )(pick, returned, first)


def forward_backward(chip_weights, rows_in, grads_in):
    n_chip = lax.axis_size(CHIPS)
    width_dev = chip_weights.shape[1] // 3
    bf16 = jnp.bfloat16
    pre_part = jnp.dot(rows_in, chip_weights[:, : 2 * width_dev], preferred_element_type=jnp.float32)
    grad_part = jnp.dot(grads_in, chip_weights[:, 2 * width_dev :], preferred_element_type=jnp.float32)
    parts = jnp.concatenate((pre_part, grad_part), axis=1).astype(bf16)
    if n_chip > 4:
        sums = exchange(parts.reshape(n_chip, -1, parts.shape[1]), CHIPS)
        sums = jnp.sum(sums.astype(jnp.float32), axis=0).astype(bf16)
        sums = lax.all_gather(sums, CHIPS, axis=0, tiled=True).astype(jnp.float32)
    else:
        sums = jnp.sum(lax.all_gather(parts, CHIPS[::-1], axis=0).astype(jnp.float32), axis=0)
    gate_pre = sums[:, :width_dev]
    up_pre = sums[:, width_dev : 2 * width_dev]
    hidden_grad = sums[:, 2 * width_dev :]
    sigma = jax.nn.sigmoid(gate_pre)
    active_part = gate_pre * sigma
    hidden = active_part * up_pre
    gate_grad = hidden_grad * up_pre * sigma * (1.0 + gate_pre * (1.0 - sigma))
    up_grad = hidden_grad * active_part
    acts = jnp.concatenate((gate_grad, up_grad, hidden), axis=1).astype(bf16)
    part_rows = lax.dot_general(
        acts[:, : 2 * width_dev],
        chip_weights[:, : 2 * width_dev],
        (((1,), (1,)), ((), ())),
        preferred_element_type=jnp.float32,
    ).astype(bf16)
    return acts, part_rows


def weight_grads(rows_in, grads_in, acts, own_depth):
    width_dev = acts.shape[1] // 3
    across = (((0,), (0,)), ((), ()))
    proj_grad = lax.dot_general(
        rows_in, acts[:, : 2 * width_dev], across, preferred_element_type=jnp.float32
    )
    down_grad = lax.dot_general(
        grads_in, acts[:, 2 * width_dev :], across, preferred_element_type=jnp.float32
    )
    grad = jnp.concatenate((proj_grad, down_grad), axis=1)
    low, high = grad[:own_depth], grad[own_depth:]
    core = lax.axis_index("core")
    other = lax.ppermute(
        jnp.where(core == 0, high, low).astype(jnp.bfloat16), "core", [(0, 1), (1, 0)]
    )
    return grad, other


def send_back(part_rows, axes):
    return exchange(part_rows.reshape(lax.axis_size(axes), CAP, part_rows.shape[1]), axes)


def add_up(returned, dest_token):
    n_chip, depth = lax.axis_size(CHIPS), returned.shape[-1]
    returned = returned.reshape(n_chip, -1, depth).transpose(1, 0, 2).reshape(-1, n_chip * depth)
    return lax.dot_general(
        dest_token, returned, (((0,), (0,)), ((), ())), preferred_element_type=jnp.float32
    ).astype(jnp.bfloat16)


def always(case, part, *operands):
    shapes = jax.eval_shape(part, *operands)
    nothing = lambda *_: tuple(jnp.zeros(shape.shape, shape.dtype) for shape in shapes)
    return lax.cond(case >= 0, part, nothing, *operands)


def one_window(pair, case, routes, gates, tokens, cotangent, weights, first_moment, second_moment):
    low, high = pair
    own_index = lax.axis_index("expert")
    active = (own_index == low) | (own_index == high)
    move = lambda block: lax.ppermute(block, "expert", [(low, high), (high, low)])
    bf16 = jnp.bfloat16
    first, second = first_moment[0], second_moment[0]
    depth = 2 * first.shape[0]

    block = jnp.where(active, move(weights[0]), weights[0])
    chip_weights = lax.all_gather(block, "core", axis=0, tiled=True)
    sends, pick = pick_rows(routes, gates, tokens, cotangent)
    got = exchange(sends.reshape(-1, 2 * CAP, depth), MIXED)
    moments = jnp.concatenate((first, second)).astype(bf16)
    chip_weights, moments = lax.optimization_barrier((chip_weights, moments))
    rows_in = got[:, :CAP].reshape(-1, depth)
    grads_in = got[:, CAP:].reshape(-1, depth)
    mid = move(moments)
    acts, part_rows = always(case, forward_backward, chip_weights, rows_in, grads_in)
    returned = send_back(part_rows, MIXED)
    acts, got = lax.optimization_barrier((acts, got))
    grad = own_grads(got, sibling(got), acts, sibling(acts))
    new_first, new_second = update(active, first, second, mid, grad)
    returned = returned.reshape(-1, depth)
    return combine(pick, returned, new_first), new_first[None], new_second[None]


def many_windows(tokens, cotangent, routes, gates, layout, weights, first_moment, second_moment):
    n_expert, n_chip = lax.axis_size("expert"), lax.axis_size(CHIPS)
    n_window = n_expert // HSPLIT
    own_index = lax.axis_index("expert")
    lane_ids = jnp.arange(n_expert, dtype=jnp.int32)
    placement, xor_mask, swap_on = layout[0], layout[1, 0], layout[2]
    held_slot = jnp.where(swap_on == 1, jnp.bitwise_xor(lane_ids, xor_mask), lane_ids)
    inverse = jnp.sum(
        jnp.where(placement[None, :] == lane_ids[:, None], lane_ids[None, :], 0), axis=1
    )
    slot_owner = inverse // HSPLIT
    expert_at = jnp.sum(
        jnp.where(held_slot[:, None] == lane_ids[None, :], slot_owner[None, :], 0), axis=1
    )
    active = select_lane(swap_on, lane_ids, own_index) == 1
    bf16 = jnp.bfloat16
    block = jnp.where(active, xor_rounds(weights[0], xor_mask), weights[0])
    moments = jnp.stack((first_moment[0], second_moment[0]))
    moved = xor_rounds(moments.astype(bf16), xor_mask).astype(jnp.float32)
    moments = jnp.where(active, moved, moments)

    tok_dev, top_count = routes.shape
    own_depth = weights.shape[1]
    depth = 2 * own_depth
    flat_ids = routes.reshape(-1)
    window_ids = jnp.arange(n_window, dtype=jnp.int32)
    hit_table = (flat_ids[:, None] == window_ids[None, :]).astype(jnp.int32)
    earlier = jnp.cumsum(hit_table, axis=0) - hit_table
    position = jnp.sum(earlier * hit_table, axis=1)
    kept = (flat_ids < n_window) & (position < CAP)
    slot_key = jnp.where(kept, flat_ids * CAP + position, -1)
    slot_pick = (jnp.arange(n_window * CAP, dtype=jnp.int32)[:, None] == slot_key[None, :]).astype(
        jnp.float32
    )
    assign_pick = slot_pick.reshape(n_window * CAP, tok_dev, top_count)
    slot_token = jnp.sum(assign_pick, axis=2)
    slot_gate = jnp.sum(assign_pick * gates[None], axis=(1, 2))[:, None]
    rows = jnp.dot(slot_token.astype(bf16), tokens, preferred_element_type=jnp.float32).astype(bf16)
    grads = jnp.dot(slot_token.astype(bf16), cotangent, preferred_element_type=jnp.float32)
    grads = (grads * slot_gate).astype(bf16)
    sends = jnp.stack((rows, grads)).reshape(2, n_window, CAP, n_chip, depth)
    sends = jnp.take(sends.transpose(3, 1, 0, 2, 4), expert_at, axis=1)
    dest_token = jnp.take(slot_token.reshape(n_window, CAP, tok_dev), expert_at, axis=0)
    dest_token = dest_token.reshape(n_expert * CAP, tok_dev).astype(bf16)
    got = exchange(sends.reshape(-1, 2 * CAP, depth), ACROSS)
    rows_in = got[:, :CAP].reshape(-1, depth)
    grads_in = got[:, CAP:].reshape(-1, depth)

    chip_weights = lax.all_gather(block, "core", axis=0, tiled=True)
    acts, part_rows = forward_backward(chip_weights, rows_in, grads_in)
    grad_input = add_up(send_back(part_rows, ACROSS), dest_token)
    grad, other = weight_grads(rows_in, grads_in, acts, own_depth)
    core = lax.axis_index("core")
    grad = jnp.where(core == 0, grad[:own_depth], grad[own_depth:]) + other.astype(jnp.float32)
    new_first = first_decay * moments[0] + (1.0 - first_decay) * grad
    new_second = second_decay * moments[1] + (1.0 - second_decay) * grad * grad
    return grad_input, new_first[None], new_second[None]


def local(tokens, cotangent, routes, gates, layout, weights, first_moment, second_moment):
    if lax.axis_size("expert") != HSPLIT:
        return many_windows(
            tokens, cotangent, routes, gates, layout, weights, first_moment, second_moment
        )
    case = swapping_pair(layout)
    branches = [functools.partial(one_window, pair) for pair in PAIRS]
    return lax.switch(
        case, branches, case, routes, gates, tokens, cotangent, weights, first_moment, second_moment
    )


def solution(mesh):
    n_dp, n_expert = mesh.devices.shape
    split = Mesh(mesh.devices.reshape(n_dp // 4, 2, 2, n_expert), ROWS)
    in_specs = (
        P(ROWS, None),
        P(ROWS, None),
        P(ROWS, None),
        P(ROWS, None),
        P(),
        P("expert", DP, None),
        P("expert", DP, None),
        P("expert", DP, None),
    )
    out_specs = (P(ROWS, None), P("expert", DP, None), P("expert", DP, None))
    return jax.shard_map(local, mesh=split, in_specs=in_specs, out_specs=out_specs, check_vma=False)
```
